128 devices in a mesh: slab: 16 (over x, z_hi, core), grp: 8 (over y, z_lo).
Axes of the slice: x: 4, y: 4, z: 4 (z_hi: 2, z_lo: 2; z = z_hi * 2 + z_lo), core: 2. Of those that a mesh axis runs over, the one named last changes fastest.
Arguments:
- src_pos: float32 [16, 8, 3, 4096], P('slab', 'grp'), may hold values from 0 to 1
- src_vort: float32 [16, 8, 3, 4096], P('slab', 'grp'), may hold values from -6 to 6
- face_valid: int32 [16, 8, 2, 2048], P('slab', 'grp'), may hold values 0 or 1
- tgt_pos: float32 [16, 8, 3, 128], P('slab', 'grp'), may hold values from 0 to 1
- tgt_vort: float32 [16, 8, 3, 128], P('slab', 'grp'), may hold values from -6 to 6
- mig_pos: float32 [16, 8, 3, 96], P('slab', 'grp'), may hold values from 0 to 1
- mig_vort: float32 [16, 8, 3, 96], P('slab', 'grp'), may hold values from -6 to 6
- mig_valid: int32 [16, 8, 96], P('slab', 'grp'), may hold values 0 or 1
- mig_route: int32 [16, 8, 96, 1], P('slab', 'grp'), may hold values from 0 to 15; in each aligned block of 96 rows (0 to 95, 96 to 191, ..., all dimensions but the last counted through in order) at most 8 rows name the same one
Outputs:
- moved_pos: float32 [16, 8, 3, 256], P('slab', 'grp')
- moved_vort: float32 [16, 8, 3, 256], P('slab', 'grp')
The draws below stay inside these ranges and needn't reach their ends.
Inputs may be any that keep to these rules, and one draw needn't show every extreme that they name: `mig_route`: value d sends a row to member d mod 8 of the slab below when d < 8, else of the slab above; the rows of one device name one value at most 8 times, and some device reaches 8.
All inputs are finite; a program needn't handle non-finite values. No bound on the sum of `face_valid` or of `mig_valid` on one device may be relied on, other than what follows from the above.
Results may differ from the reference program's by a relative error of at most 0.00065.
Values sent between devices are 32-bit elements; how exact they have to be, the bound alone decides.
No kernel may reach another device: no remote copies, remote signals or barrier semaphores. Data moves between devices by JAX's collectives and lax.ppermute only.
A program may use at most 128 MiB of HBM per device.

```python
import math
from functools import partial
import jax
import jax.numpy as jnp
import numpy as np
from jax import lax

SRC = 4096
TGT = 128
CAP = 8
STEPS = 2
FACE = 2048
MIG = 96
N_SLAB = 16
N_GRP = 8


def place_ends(drawn, key, least, top_value):
    place = [jax.random.randint(jax.random.fold_in(key, axis), (), 0, length) for axis, length in enumerate(drawn.shape)]
    main_axis = drawn.shape.index(max(drawn.shape))
    neighbour = place[:main_axis] + [(place[main_axis] + 1) % drawn.shape[main_axis]] + place[main_axis + 1:]
    return drawn.at[tuple(place)].set(least).at[tuple(neighbour)].set(top_value)


def level_of(stream_key, dims, pieces, low, top_value):
    def one(position, blocks):
        draws = jax.random.uniform(jax.random.fold_in(jax.random.fold_in(stream_key, 6), position), (blocks,), jnp.float32, low / len(pieces), top_value / len(pieces))
        return jnp.repeat(jnp.exp(draws), dims[position] // blocks).reshape((-1,) + (1,) * (len(dims) - position - 1))

    loudness = one(*pieces[0])
    for cut in pieces[1:]:
        loudness = loudness * one(*cut)
    return loudness


def routed_block(own_key, own, number, rows, number_of, top, reach, skew):
    order = jax.random.permutation(own_key, number_of)
    packed, ordinary = portions_of(number_of, rows * top, reach, skew, True), portions_of(number_of, rows * top, reach, skew, False)
    places = jnp.arange(number_of)

    def named(lengths, rotation):
        used = int((lengths > 0).sum())
        fixed = max(1, used // 4)
        moved = fixed + (places - fixed + rotation * (used - fixed)) % max(1, number_of - fixed)
        return jnp.zeros((number_of,), jnp.int32).at[order[jnp.where(places < fixed, places, moved)]].set(jnp.asarray(lengths, jnp.int32))

    lengths = jnp.where(number % 4 == 0, named(packed, number // 4), named(ordinary, number - number // 4 - 1))
    mixed = jax.random.permutation(jax.random.fold_in(own, 3), number_of)
    source_of, taker = mixed[0:number_of // 2 * 2:2], mixed[1:number_of // 2 * 2:2]
    margin = jnp.minimum(lengths[source_of] - 1, reach - lengths[taker]) // 2
    margin = jnp.where((source_of == order[0]) | (taker == order[0]) | (lengths[taker] == 0), 0, jnp.maximum(margin, 0))
    moved = jax.random.randint(jax.random.fold_in(own, 4), (number_of // 2,), 0, 1 << 20) % (margin + 1)
    lengths = lengths.at[source_of].add(-moved).at[taker].add(moved)
    members = jnp.searchsorted(jnp.cumsum(lengths), jnp.arange(rows * top), side="right").astype(jnp.int32)
    table = members.reshape(top, rows).T
    table = table[jax.random.permutation(jax.random.fold_in(own, 1), rows)]
    rotation = jax.random.randint(jax.random.fold_in(own, 2), (rows, 1), 0, top)
    return jnp.take_along_axis(table, (jnp.arange(top)[None, :] + rotation) % top, axis=1)


def portions_of(amount, total, limit, lean, full):
    loads = [(1 << 20) // math.isqrt(grade ** lean) + 1 for grade in range(1, amount + 1)]
    largest = limit if full else min(limit, max(-(-total // amount), total * loads[0] // sum(loads)))
    least = 1 if total - largest >= amount - 1 else 0
    given, rest = [largest] + [least] * (amount - 1), total - largest - least * (amount - 1)
    while rest > 0:
        free = [i for i in range(1, amount) if given[i] < largest] or [i for i in range(1, amount) if given[i] < limit]
        mass, budget = sum([loads[i] for i in free]), rest
        for i in free:
            addition = min(limit - given[i], max(1, budget * loads[i] // mass), rest)
            given[i] = given[i] + addition
            rest = rest - addition
    return np.array(given)


def normal_values(key, shape, width, reach, split=(), kind=jnp.bfloat16):
    level = level_of(key, shape, split, -0.22, 0.18) if split else 1.0
    result = jax.random.normal(key, shape, jnp.float32) * width * level
    return jnp.minimum(jnp.maximum(result, -reach), reach).astype(kind)


def setup_inputs(seed: int = 0) -> dict:
    arg_keys = jax.random.split(jax.random.key(seed), 10)
    src_pos = jnp.clip(1.0 * jax.random.uniform(arg_keys[0], (N_SLAB, N_GRP, 3, SRC), jnp.float32) ** level_of(arg_keys[0], (N_SLAB, N_GRP, 3, SRC), ((0, 16), (1, 8)), -0.2, 0.2), 0.0, 1.0)
    src_vort = normal_values(arg_keys[1], (N_SLAB, N_GRP, 3, SRC), 1.0, 6.0, ((0, 16), (1, 8)), jnp.float32)
    face_valid = place_ends((jax.random.randint(arg_keys[2], (N_SLAB, N_GRP, 2, FACE), 0, 8) < 7).astype(jnp.int32), jax.random.fold_in(arg_keys[2], 1), 0, 1)
    tgt_pos = jnp.clip(1.0 * jax.random.uniform(arg_keys[3], (N_SLAB, N_GRP, 3, TGT), jnp.float32) ** level_of(arg_keys[3], (N_SLAB, N_GRP, 3, TGT), ((0, 16), (1, 8)), -0.2, 0.2), 0.0, 1.0)
    tgt_vort = normal_values(arg_keys[4], (N_SLAB, N_GRP, 3, TGT), 1.0, 6.0, ((0, 16), (1, 8)), jnp.float32)
    mig_pos = jnp.clip(1.0 * jax.random.uniform(arg_keys[5], (N_SLAB, N_GRP, 3, MIG), jnp.float32) ** level_of(arg_keys[5], (N_SLAB, N_GRP, 3, MIG), ((0, 16), (1, 8)), -0.2, 0.2), 0.0, 1.0)
    mig_vort = normal_values(arg_keys[6], (N_SLAB, N_GRP, 3, MIG), 1.0, 6.0, ((0, 16), (1, 8)), jnp.float32)
    mig_valid = place_ends((jax.random.randint(arg_keys[7], (N_SLAB, N_GRP, MIG), 0, 4) < 3).astype(jnp.int32), jax.random.fold_in(arg_keys[7], 1), 0, 1)
    mig_route_keys = jax.random.split(jax.random.fold_in(arg_keys[8], 1), N_SLAB * N_GRP * MIG // MIG)
    mig_route_turns = jax.random.permutation(jax.random.fold_in(arg_keys[8], 3), N_SLAB * N_GRP * MIG // MIG)
    mig_route = jax.vmap(lambda own, number: routed_block(jax.random.fold_in(arg_keys[8], 2), own, number, MIG, 2 * N_GRP, 1, CAP, 2))(mig_route_keys, mig_route_turns).reshape((N_SLAB, N_GRP, MIG, 1))
    return dict(src_pos=src_pos, src_vort=src_vort, face_valid=face_valid, tgt_pos=tgt_pos, tgt_vort=tgt_vort, mig_pos=mig_pos, mig_vort=mig_vort, mig_valid=mig_valid, mig_route=mig_route)


core_square = 0.0225
time_step = 0.1
strength = 0.03 / (4.0 * math.pi)
highest = lax.Precision.HIGHEST

def expand(places, vortex):
    length = places.shape[1]
    squares = lax.optimization_barrier(jnp.sum(places * places, axis=0, keepdims=True))
    curled = jnp.cross(places, vortex, axis=0)
    outer_vort = (places[:, None, :] * vortex[None, :, :]).reshape(9, length)
    outer_curl = (places[:, None, :] * curled[None, :, :]).reshape(9, length)
    return jnp.concatenate([places, squares, vortex, curled, outer_vort, outer_curl], axis=0)

def field_sums(where_pos, where_sq, features):
    length = features.shape[1]
    block_width = math.gcd(length, 4096)

    def one_block(iteration, running):
        block = lax.dynamic_slice_in_dim(features, iteration * block_width, block_width, 1)
        inner_dot = lax.dot_general(block[0:3], where_pos, (((0,), (0,)), ((), ())), precision=highest, preferred_element_type=jnp.float32)
        distance = block[3][:, None] + where_sq[None, :] - 2.0 * inner_dot
        inverse = 1.0 / (distance + core_square)
        root_inv = jnp.sqrt(inverse)
        qweight = (distance + 2.5 * core_square) * inverse * inverse * root_inv
        fweight = -(3.0 * distance + 10.5 * core_square) * inverse * inverse * inverse * root_inv
        near_sums = jnp.dot(block[4:10], qweight, precision=highest, preferred_element_type=jnp.float32)
        grad_sums = jnp.dot(block[4:28], fweight, precision=highest, preferred_element_type=jnp.float32)
        return running + jnp.concatenate([near_sums, grad_sums], axis=0)
    start = jnp.zeros((30, where_pos.shape[1]), jnp.float32)
    return lax.fori_loop(0, length // block_width, one_block, start)

def rates_from(where_pos, where_vort, blocks):
    where_sq = lax.optimization_barrier(jnp.sum(where_pos * where_pos, axis=0))
    sums = field_sums(where_pos, where_sq, blocks[0])
    for extra in blocks[1:]:
        sums = sums + field_sums(where_pos, where_sq, extra)
    count = where_pos.shape[1]
    near_vort = sums[0:3]
    near_curl = sums[3:6]
    grad_vort = sums[6:9]
    grad_curl = sums[9:12]
    grad_outer_vort = sums[12:21].reshape(3, 3, count)
    grad_outer_curl = sums[21:30].reshape(3, 3, count)
    velocity = -strength * (jnp.cross(where_pos, near_vort, axis=0) - near_curl)
    along = lax.optimization_barrier(jnp.sum(where_vort * where_pos, axis=0))
    first_term = along[None, :] * (jnp.cross(where_pos, grad_vort, axis=0) - grad_curl)
    inside = jnp.cross(where_pos[None, :, :], grad_outer_vort, axis=1) - grad_outer_curl
    second_term = lax.optimization_barrier(jnp.sum(where_vort[:, None, :] * inside, axis=0))
    stretch = -strength * (jnp.cross(where_vort, near_vort, axis=0) + first_term - second_term)
    return (velocity, stretch)

def buckets(mig_pos, mig_vort, mig_valid, routing, groups, capacity):
    destinations = 2 * groups
    matches = (routing[:, 0][:, None] == jnp.arange(destinations, dtype=jnp.int32)[None, :]).astype(jnp.int32)
    before = jnp.cumsum(matches, axis=0) - matches
    order_in = lax.optimization_barrier(jnp.sum(before * matches, axis=1))
    slot_index = routing[:, 0] * capacity + order_in
    placing = (slot_index[:, None] == jnp.arange(destinations * capacity, dtype=jnp.int32)[None, :]).astype(jnp.float32)
    record = jnp.concatenate([mig_pos, mig_vort, mig_valid.astype(jnp.float32)[None, :]], axis=0)
    placed = jnp.dot(record, placing, precision=highest, preferred_element_type=jnp.float32)
    return placed.reshape(7, 2, groups, capacity)

def frame_table():
    first = (jnp.arange(7, dtype=jnp.int32) == 0).astype(jnp.float32)[:, None]
    sides = jnp.array([-1.0, 1.0], dtype=jnp.float32)[None, :]
    return first * sides

def reference(src_pos, src_vort, face_valid, tgt_pos, tgt_vort, mig_pos, mig_vort, mig_valid, mig_route):
    slabs = src_pos.shape[0]
    groups = src_pos.shape[1]
    face_count = face_valid.shape[3]
    along_jet = (jnp.arange(3, dtype=jnp.int32) == 0).astype(jnp.float32)[:, None]
    face_masks = face_valid.astype(jnp.float32)
    filled = jax.vmap(jax.vmap(partial(buckets, groups=groups, capacity=CAP)))(mig_pos, mig_vort, mig_valid, mig_route)
    from_lower = jnp.roll(filled[:, :, :, 1], 1, axis=0)
    from_upper = jnp.roll(filled[:, :, :, 0], -1, axis=0)
    arrived = jnp.stack([from_lower, from_upper], axis=3)
    arrived = arrived.transpose(0, 4, 2, 3, 1, 5)
    arrived = arrived + frame_table()[None, None, :, :, None, None]
    where_pos = jnp.concatenate([tgt_pos, arrived[:, :, 0:3].reshape(slabs, groups, 3, -1)], axis=3)
    where_vort = jnp.concatenate([tgt_vort, arrived[:, :, 3:6].reshape(slabs, groups, 3, -1)], axis=3)
    living = jnp.concatenate([jnp.ones(tgt_pos.shape[0:2] + (tgt_pos.shape[3],), jnp.float32), arrived[:, :, 6].reshape(slabs, groups, -1)], axis=2)

    def by_slab(values):
        return values.transpose(0, 2, 1, 3).reshape(slabs, 3, -1)
    low_pos = by_slab(src_pos[:, :, :, :face_count] + along_jet[None, None])
    low_vort = by_slab(src_vort[:, :, :, :face_count] * face_masks[:, :, 0][:, :, None, :])
    high_pos = by_slab(src_pos[:, :, :, -face_count:] - along_jet[None, None])
    high_vort = by_slab(src_vort[:, :, :, -face_count:] * face_masks[:, :, 1][:, :, None, :])
    slab_pos = jnp.concatenate([by_slab(src_pos), jnp.roll(high_pos, 1, axis=0), jnp.roll(low_pos, -1, axis=0)], axis=2)
    slab_vort = jnp.concatenate([by_slab(src_vort), jnp.roll(high_vort, 1, axis=0), jnp.roll(low_vort, -1, axis=0)], axis=2)

    def device_run(items):
        place_one, vort_one, slab_index = items
        pos_all = lax.dynamic_index_in_dim(slab_pos, slab_index, 0, keepdims=False)
        vort_all = lax.dynamic_index_in_dim(slab_vort, slab_index, 0, keepdims=False)
        features = expand(pos_all, vort_all)
        for substep in range(STEPS):
            velocity, stretch = rates_from(place_one, vort_one, (features,))
            place_one = place_one + time_step * velocity
            vort_one = vort_one + time_step * stretch
        return (place_one, vort_one)
    slab_ids = jnp.repeat(jnp.arange(slabs, dtype=jnp.int32), groups)
    count = where_pos.shape[3]
    moved_pos, moved_vort = lax.map(device_run, (where_pos.reshape(slabs * groups, 3, count), where_vort.reshape(slabs * groups, 3, count), slab_ids))
    moved_pos = moved_pos.reshape(slabs, groups, 3, count) * living[:, :, None, :]
    moved_vort = moved_vort.reshape(slabs, groups, 3, count) * living[:, :, None, :]
    return (moved_pos, moved_vort)
```

```python
import functools
import math

import jax
import jax.numpy as jnp
from jax import lax
from jax.experimental import pallas as pl
from jax.experimental.pallas import tpu as pltpu
from jax.sharding import PartitionSpec as P

CAP = 8
STEPS = 2
core_square = 0.0225
time_step = 0.1
strength = 0.03 / (4.0 * math.pi)
highest = lax.Precision.HIGHEST

centre = 0.5
unit_square = 1.5 * core_square
unit = math.sqrt(unit_square)
velocity_factor = -strength / unit_square
stretch_factor = -strength / (unit_square * unit)
f32 = jnp.float32
bf16 = jnp.bfloat16
BLOCK = 4096


def three_pieces(values):
    high = values.astype(bf16).astype(f32)
    rest = values - high
    middle = rest.astype(bf16).astype(f32)
    low = rest - middle
    return high, middle, low


def prepare_kernel(pos_ref, vort_ref, near_ref, grad_ref, dist_ref, rows, dist):
    places = [(pos_ref[k : k + 1, :] - centre) * (1.0 / unit) for k in range(3)]
    vortex = [vort_ref[k : k + 1, :] for k in range(3)]
    curled = [
        places[(k + 1) % 3] * vortex[(k + 2) % 3] - places[(k + 2) % 3] * vortex[(k + 1) % 3]
        for k in range(3)
    ]
    for k in range(3):
        rows[k : k + 1, :] = vortex[k]
        rows[3 + k : 4 + k, :] = curled[k]
        for l in range(3):
            at = 6 + 3 * k + l
            rows[at : at + 1, :] = places[k] * vortex[l]
            rows[at + 9 : at + 10, :] = places[k] * curled[l]
    high, middle, low = three_pieces(rows[...])
    blank = jnp.zeros((8, high.shape[1]), f32)
    grad_ref[...] = jnp.concatenate([high, middle, low, blank], axis=0).astype(bf16)
    near_ref[...] = jnp.concatenate([high[0:8], middle[0:8], low[0:8], blank], axis=0).astype(bf16)
    square = places[0] * places[0] + places[1] * places[1] + places[2] * places[2]
    square_parts = three_pieces(square + core_square / unit_square)
    dist[...] = jnp.zeros_like(dist)
    for k in range(3):
        parts = three_pieces(places[k])
        for place, part in enumerate((0, 0, 1, 0, 2, 1)):
            dist[3 * place + k : 3 * place + k + 1, :] = parts[part]
        dist[18 + k : 19 + k, :] = square_parts[k]
        dist[21 + k : 22 + k, :] = jnp.ones_like(square)
    dist_ref[...] = dist[...].astype(bf16)


def prepare(places, vortex):
    length = places.shape[1]
    whole = pl.BlockSpec(memory_space=pltpu.VMEM)
    return pl.pallas_call(
        prepare_kernel,
        in_specs=[whole, whole],
        out_specs=[whole, whole, whole],
        out_shape=[
            jax.ShapeDtypeStruct((32, length), bf16),
            jax.ShapeDtypeStruct((80, length), bf16),
            jax.ShapeDtypeStruct((32, length), bf16),
        ],
        scratch_shapes=[pltpu.VMEM((24, length), f32), pltpu.VMEM((32, length), f32)],
        compiler_params=pltpu.CompilerParams(vmem_limit_bytes=48 << 20),
    )(places, vortex)


def two_pieces(values):
    high = values.astype(bf16)
    low = (values - high.astype(f32)).astype(bf16)
    return jnp.concatenate([high, low], axis=0)


def dot(left, right):
    return lax.dot_general(left, right, (((1,), (0,)), ((), ())), preferred_element_type=f32)


def cross(left, right):
    return [
        left[(k + 1) % 3] * right[(k + 2) % 3] - left[(k + 2) % 3] * right[(k + 1) % 3]
        for k in range(3)
    ]


def pairs_kernel(tgt_ref, near_ref, grad_ref, dist_ref, out_ref, tgt, near_sums, grad_sums):
    where = [(tgt_ref[0, k : k + 1, :] - centre) * (1.0 / unit) for k in range(3)]
    vortex = [tgt_ref[0, 3 + k : 4 + k, :] for k in range(3)]
    square = where[0] * where[0] + where[1] * where[1] + where[2] * where[2]
    square_parts = three_pieces(square)
    tgt[...] = jnp.zeros_like(tgt)
    for k in range(3):
        parts = three_pieces(-2.0 * where[k])
        for place, part in enumerate((0, 1, 0, 2, 0, 1)):
            tgt[3 * place + k : 3 * place + k + 1, :] = parts[part]
        tgt[18 + k : 19 + k, :] = jnp.ones_like(square)
        tgt[21 + k : 22 + k, :] = square_parts[k]
    targets = tgt[...].astype(bf16)
    near_sums[...] = jnp.zeros_like(near_sums)
    grad_sums[...] = jnp.zeros_like(grad_sums)
    length = near_ref.shape[1]
    width = min(BLOCK, length)

    def one_block(index, carry):
        piece = pl.ds(pl.multiple_of(index * width, width), width)
        distance = lax.dot_general(
            dist_ref[:, piece], targets, (((0,), (0,)), ((), ())), preferred_element_type=f32
        )
        root = lax.rsqrt(distance)
        square_inv = root * root
        third = square_inv * root
        fifth = third * square_inv
        qweight = two_pieces(third + fifth)
        fweight = two_pieces(fifth * (square_inv + 0.6))
        near = near_ref[:, piece]
        grad = grad_ref[:, piece]
        near_sums[...] += dot(jnp.concatenate([near, near], axis=1), qweight)
        grad_sums[...] += dot(jnp.concatenate([grad, grad], axis=1), fweight)
        return carry

    lax.fori_loop(0, length // width, one_block, 0)
    near = near_sums[0:8, :] + near_sums[8:16, :] + near_sums[16:24, :]
    grad = grad_sums[0:24, :] + grad_sums[24:48, :] + grad_sums[48:72, :]

    def three(values, first):
        return [values[first + k : first + k + 1, :] for k in range(3)]

    near_vort, near_curl = three(near, 0), three(near, 3)
    grad_vort, grad_curl = three(grad, 0), three(grad, 3)
    turned = cross(where, near_vort)
    velocity = [velocity_factor * (turned[k] - near_curl[k]) for k in range(3)]
    along = vortex[0] * where[0] + vortex[1] * where[1] + vortex[2] * where[2]
    turned = cross(where, grad_vort)
    inner = [along * (turned[k] - grad_curl[k]) for k in range(3)]
    for axis in range(3):
        turned = cross(where, three(grad, 6 + 3 * axis))
        outer = three(grad, 15 + 3 * axis)
        inner = [inner[k] - vortex[axis] * (turned[k] - outer[k]) for k in range(3)]
    turned = cross(vortex, near_vort)
    out_ref[...] = jnp.zeros_like(out_ref)
    for k in range(3):
        out_ref[0, k : k + 1, :] = velocity[k]
        out_ref[0, 3 + k : 4 + k, :] = stretch_factor * (turned[k] - 5.0 * inner[k])


def pair_sums(table, near, grad, dist):
    tiles, rows, width = table.shape
    whole = pl.BlockSpec(memory_space=pltpu.VMEM)
    return pl.pallas_call(
        pairs_kernel,
        grid=(tiles,),
        in_specs=[pl.BlockSpec((1, rows, width), lambda i: (i, 0, 0)), whole, whole, whole],
        out_specs=pl.BlockSpec((1, rows, width), lambda i: (i, 0, 0)),
        out_shape=jax.ShapeDtypeStruct(table.shape, f32),
        scratch_shapes=[
            pltpu.VMEM((32, width), f32),
            pltpu.VMEM((32, width), f32),
            pltpu.VMEM((80, width), f32),
        ],
        compiler_params=pltpu.CompilerParams(vmem_limit_bytes=56 << 20),
    )(table, near, grad, dist)


def buckets(mig_pos, mig_vort, mig_valid, routing, groups, capacity):
    destinations = 2 * groups
    matches = (routing[:, 0][:, None] == jnp.arange(destinations, dtype=jnp.int32)[None, :]).astype(
        jnp.int32
    )
    before = jnp.cumsum(matches, axis=0) - matches
    order_in = jnp.sum(before * matches, axis=1)
    slot_index = routing[:, 0] * capacity + order_in
    placing = (
        slot_index[:, None] == jnp.arange(destinations * capacity, dtype=jnp.int32)[None, :]
    ).astype(f32)
    record = jnp.concatenate([mig_pos, mig_vort, mig_valid.astype(f32)[None, :]], axis=0)
    placed = jnp.dot(record, placing, precision=highest, preferred_element_type=f32)
    return placed.reshape(7, 2, groups * capacity)


def swap(values):
    return lax.all_to_all(values, "grp", split_axis=0, concat_axis=0, tiled=True)


def spread(values, groups):
    return swap(jnp.broadcast_to(values[None], (groups,) + values.shape))


def per_device(
    src_pos, src_vort, face_valid, tgt_pos, tgt_vort, mig_pos, mig_vort, mig_valid, mig_route
):
    groups = lax.axis_size("grp")
    slabs = lax.axis_size("slab")
    member = lax.axis_index("grp")
    places = src_pos[0, 0]
    vortex = src_vort[0, 0]
    sources = places.shape[1]
    faces = face_valid.shape[3]
    own = tgt_pos.shape[3]
    masks = face_valid[0, 0].astype(f32)
    along_jet = (jnp.arange(3, dtype=jnp.int32) == 0).astype(f32)[:, None]
    filled = buckets(mig_pos[0, 0], mig_vort[0, 0], mig_valid[0, 0], mig_route[0, 0], groups, CAP)
    slots = filled.shape[2]
    shift = (jnp.arange(7, dtype=jnp.int32) == 0).astype(f32)[:, None]
    going_up = jnp.concatenate(
        [
            jnp.concatenate([places[:, sources - faces :] - along_jet], axis=0).reshape(-1),
            (vortex[:, sources - faces :] * masks[1][None]).reshape(-1),
            (filled[:, 1] - shift).reshape(-1),
        ]
    )
    going_down = jnp.concatenate(
        [
            (places[:, :faces] + along_jet).reshape(-1),
            (vortex[:, :faces] * masks[0][None]).reshape(-1),
            (filled[:, 0] + shift).reshape(-1),
        ]
    )
    from_lower = lax.ppermute(going_up, "slab", [(i, (i + 1) % slabs) for i in range(slabs)])
    from_upper = lax.ppermute(going_down, "slab", [((i + 1) % slabs, i) for i in range(slabs)])
    arrived = jnp.stack([from_lower[6 * faces :], from_upper[6 * faces :]])
    arrived = arrived.reshape(2, 7, groups, CAP).transpose(1, 2, 0, 3).reshape(-1)
    sent = jnp.concatenate([tgt_pos[0, 0].reshape(-1), tgt_vort[0, 0].reshape(-1), arrived])
    table = spread(sent.reshape(-1, 128), groups).reshape(groups, -1)
    own_part = table[:, : 6 * own].reshape(groups, 6, own)
    own_part = jnp.concatenate(
        [own_part, jnp.ones((groups, 1, own), f32), jnp.zeros((groups, 1, own), f32)], axis=1
    )
    slot_part = table[:, 6 * own :].reshape(groups, 7, groups, 2, CAP).transpose(2, 1, 3, 0, 4)
    slot_part = slot_part.reshape(groups, 7, 2 * groups * CAP)
    slot_part = jnp.pad(slot_part, ((0, 0), (0, 1), (0, 0)))
    table = jnp.concatenate([own_part, slot_part], axis=2)

    all_places = jnp.concatenate(
        [places, from_lower[: 3 * faces].reshape(3, faces), from_upper[: 3 * faces].reshape(3, faces)],
        axis=1,
    )
    all_vortex = jnp.concatenate(
        [
            vortex,
            from_lower[3 * faces : 6 * faces].reshape(3, faces),
            from_upper[3 * faces : 6 * faces].reshape(3, faces),
        ],
        axis=1,
    )
    near, grad, dist = prepare(all_places, all_vortex)
    mine = lax.dynamic_index_in_dim(table, member, 0, keepdims=False)
    living = mine[6:7]
    for substep in range(STEPS):
        if substep > 0:
            table = spread(mine, groups)
        partial = swap(pair_sums(table, near, grad, dist))
        mine = mine + time_step * jnp.sum(partial, axis=0)
    moved_pos = (mine[0:3] * living)[None, None]
    moved_vort = (mine[3:6] * living)[None, None]
    return (moved_pos, moved_vort)


def solution(mesh):
    return jax.shard_map(
        per_device,
        mesh=mesh,
        in_specs=(
            P("slab", "grp", None, None),
            P("slab", "grp", None, None),
            P("slab", "grp", None, None),
            P("slab", "grp", None, None),
            P("slab", "grp", None, None),
            P("slab", "grp", None, None),
            P("slab", "grp", None, None),
            P("slab", "grp", None),
            P("slab", "grp", None, None),
        ),
        out_specs=(P("slab", "grp", None, None), P("slab", "grp", None, None)),
        check_vma=False,
    )
```

```python
import functools
import math

import jax
import jax.numpy as jnp
from jax import lax
from jax.experimental import pallas as pl
from jax.experimental.pallas import tpu as pltpu
from jax.sharding import PartitionSpec as P

CAP = 8
STEPS = 2
core_square = 0.0225
time_step = 0.1
strength = 0.03 / (4.0 * math.pi)

centre = 0.5
unit_square = 1.5 * core_square
unit = math.sqrt(unit_square)
velocity_factor = -strength / unit_square
stretch_factor = -strength / (unit_square * unit)
f32 = jnp.float32
bf16 = jnp.bfloat16
whole = pl.BlockSpec(memory_space=pltpu.VMEM)


def three_pieces(values):
    high = values.astype(bf16).astype(f32)
    rest = values - high
    middle = rest.astype(bf16).astype(f32)
    low = rest - middle
    return high, middle, low


def two_pieces(values):
    high = values.astype(bf16)
    low = (values - high.astype(f32)).astype(bf16)
    return jnp.concatenate([high, low], axis=0)


def dot(left, right):
    return lax.dot_general(left, right, (((1,), (0,)), ((), ())), preferred_element_type=f32)


def cross(left, right):
    return [
        left[(k + 1) % 3] * right[(k + 2) % 3] - left[(k + 2) % 3] * right[(k + 1) % 3]
        for k in range(3)
    ]


def send_kernel(
    faces, pos_ref, vort_ref, valid_ref, mig_pos_ref, mig_vort_ref, mig_valid_ref, route_ref,
    up_ref, down_ref, record,
):
    sources = pos_ref.shape[1]
    migrants = route_ref.shape[0]
    slots = (up_ref.shape[1] - faces) // 2
    destinations = 2 * slots // CAP
    route = route_ref[...]
    matches = route == lax.broadcasted_iota(jnp.int32, (migrants, destinations), 1)
    matches = jnp.where(matches, 1.0, 0.0)
    earlier = lax.broadcasted_iota(jnp.int32, (migrants, migrants), 0) > lax.broadcasted_iota(
        jnp.int32, (migrants, migrants), 1
    )
    before = dot(jnp.where(earlier, 1.0, 0.0).astype(bf16), matches.astype(bf16))
    order = jnp.sum(before * matches, axis=1, keepdims=True).astype(jnp.int32)
    placing = (route * CAP + order) == lax.broadcasted_iota(jnp.int32, (migrants, 2 * slots), 1)
    placing = jnp.where(placing, 1.0, 0.0).astype(bf16)
    record[...] = jnp.zeros_like(record)
    record[0:3, :] = mig_pos_ref[...]
    record[3:6, :] = mig_vort_ref[...]
    record[6:7, :] = mig_valid_ref[...].astype(f32)
    pieces = jnp.concatenate(three_pieces(record[...]), axis=0)
    placed = dot(jnp.concatenate([pieces, jnp.zeros((8, migrants), f32)], axis=0).astype(bf16), placing)
    placed = placed[0:8] + placed[8:16] + placed[16:24]
    first = lax.broadcasted_iota(jnp.int32, placed.shape, 0) == 0
    for ref, begin, shift, which in ((down_ref, 0, 1.0, 0), (up_ref, sources - faces, -1.0, 1)):
        piece = slice(begin, begin + faces)
        mask = valid_ref[which : which + 1, :].astype(f32)
        ref[0:1, :faces] = pos_ref[0:1, piece] + shift
        ref[1:3, :faces] = pos_ref[1:3, piece]
        ref[3:6, :faces] = vort_ref[:, piece] * mask
        ref[6:8, :faces] = jnp.zeros((2, faces), f32)
        ref[:, faces:] = jnp.where(first, placed + shift, placed)


def make_sends(places, vortex, valid, mig_pos, mig_vort, mig_valid, route, destinations):
    faces = valid.shape[1]
    shape = jax.ShapeDtypeStruct((8, faces + destinations * CAP), f32)
    return pl.pallas_call(
        functools.partial(send_kernel, faces),
        in_specs=[whole] * 7,
        out_specs=[whole] * 2,
        out_shape=[shape, shape],
        scratch_shapes=[pltpu.VMEM((8, route.shape[0]), f32)],
        compiler_params=pltpu.CompilerParams(vmem_limit_bytes=48 << 20),
    )(places, vortex, valid, mig_pos, mig_vort, mig_valid, route)


def prepare_kernel(length, *refs):
    source_refs = refs[:-5]
    near_ref, grad_ref, dist_ref, rows, dist = refs[-5:]

    def columns(row):
        if source_refs[0].shape[0] == 3:
            return source_refs[row // 3][row % 3 : row % 3 + 1, :]
        return jnp.concatenate([ref[row : row + 1, : length // 2] for ref in source_refs], axis=1)

    places = [(columns(k) - centre) * (1.0 / unit) for k in range(3)]
    vortex = [columns(3 + k) for k in range(3)]
    curled = cross(places, vortex)
    for k in range(3):
        rows[k : k + 1, :] = vortex[k]
        rows[3 + k : 4 + k, :] = curled[k]
        for l in range(3):
            at = 6 + 3 * k + l
            rows[at : at + 1, :] = places[k] * vortex[l]
            rows[at + 9 : at + 10, :] = places[k] * curled[l]
    high, middle, low = three_pieces(rows[...])
    blank = jnp.zeros((8, high.shape[1]), f32)
    grad_ref[...] = jnp.concatenate([high, middle, low, blank], axis=0).astype(bf16)
    near_ref[...] = jnp.concatenate([high[0:8], middle[0:8], low[0:8], blank], axis=0).astype(bf16)
    square = places[0] * places[0] + places[1] * places[1] + places[2] * places[2]
    square_parts = three_pieces(square + core_square / unit_square)
    dist[...] = jnp.zeros_like(dist)
    for k in range(3):
        parts = three_pieces(places[k])
        for place, part in enumerate((0, 0, 1, 0, 2, 1)):
            dist[3 * place + k : 3 * place + k + 1, :] = parts[part]
        dist[18 + k : 19 + k, :] = square_parts[k]
        dist[21 + k : 22 + k, :] = jnp.ones_like(square)
    dist_ref[...] = dist[...].astype(bf16)


def prepare(length, *sources):
    return pl.pallas_call(
        functools.partial(prepare_kernel, length),
        in_specs=[whole] * len(sources),
        out_specs=[whole] * 3,
        out_shape=[
            jax.ShapeDtypeStruct((32, length), bf16),
            jax.ShapeDtypeStruct((80, length), bf16),
            jax.ShapeDtypeStruct((32, length), bf16),
        ],
        scratch_shapes=[pltpu.VMEM((24, length), f32), pltpu.VMEM((32, length), f32)],
        compiler_params=pltpu.CompilerParams(vmem_limit_bytes=48 << 20),
    )(*sources)


def compact_kernel(arrived_ref, table_ref, rank_ref, count_ref):
    groups, _, slots = arrived_ref.shape
    valid = jnp.concatenate([arrived_ref[m, 14:15, :] for m in range(groups)], axis=0)
    row = lax.broadcasted_iota(jnp.int32, (slots, slots), 0)
    column = lax.broadcasted_iota(jnp.int32, (slots, slots), 1)
    earlier = jnp.where(row < column, 1.0, 0.0).astype(bf16)
    same = jnp.where(row == column, 1.0, 0.0).astype(bf16)

    def turned(matrix, which):
        return lax.dot_general(
            matrix, which, (((0,), (1,)), ((), ())), preferred_element_type=f32
        )

    flags = valid.astype(bf16)
    within = turned(earlier, flags)
    living = turned(same, flags)
    totals = jnp.sum(living, axis=0, keepdims=True)
    ahead = [jnp.zeros((1, 1), f32)]
    for m in range(1, groups):
        ahead.append(ahead[-1] + totals[:, m - 1 : m])
    rank = jnp.where(living > 0.5, within + jnp.concatenate(ahead, axis=1), -1.0)
    rank_ref[...] = rank
    count_ref[0, 0] = jnp.sum(valid).astype(jnp.int32)
    wanted = lax.broadcasted_iota(jnp.int32, (slots, groups * slots), 1).astype(f32)
    placed = jnp.zeros((32, groups * slots), f32)
    for m in range(groups):
        pieces = three_pieces(arrived_ref[m, 8:16, :])
        pieces = jnp.concatenate(pieces + (jnp.zeros((8, slots), f32),), axis=0).astype(bf16)
        chosen = jnp.where(rank[:, m : m + 1] == wanted, 1.0, 0.0).astype(bf16)
        placed = placed + dot(pieces, chosen)
    placed = placed[0:8] + placed[8:16] + placed[16:24]
    for m in range(groups):
        table_ref[m] = placed[:, m * slots : (m + 1) * slots]


def compact(received):
    groups, _, slots = received.shape
    return pl.pallas_call(
        compact_kernel,
        in_specs=[whole],
        out_specs=[whole, whole, pl.BlockSpec(memory_space=pltpu.SMEM)],
        out_shape=[
            jax.ShapeDtypeStruct((groups, 8, slots), f32),
            jax.ShapeDtypeStruct((slots, groups), f32),
            jax.ShapeDtypeStruct((1, 1), jnp.int32),
        ],
        compiler_params=pltpu.CompilerParams(vmem_limit_bytes=48 << 20),
    )(received)


def expand_kernel(rank_ref, own_ref, moved_ref, table_ref, sums_ref, places_ref):
    groups, _, slots = moved_ref.shape
    rows = [
        jnp.concatenate([ref[m] for m in range(groups)], axis=1) for ref in (moved_ref, table_ref)
    ]
    pieces = jnp.concatenate(three_pieces(jnp.concatenate(rows, axis=0)), axis=0).astype(bf16)
    wanted = lax.broadcasted_iota(jnp.int32, (slots, groups * slots), 1).astype(f32)
    for member in range(groups):
        chosen = jnp.where(rank_ref[:, member : member + 1] == wanted, 1.0, 0.0).astype(bf16)
        found = lax.dot_general(
            pieces, chosen, (((1,), (1,)), ((), ())), preferred_element_type=f32
        )
        found = found[0:16] + found[16:32] + found[32:48]
        sums_ref[member, 0:8, :] = own_ref[member]
        sums_ref[member, 8:16, :] = found[0:8]
        places_ref[member] = found[8:16]


def expand_slots(rank, own, moved, table):
    groups, _, slots = moved.shape
    return pl.pallas_call(
        expand_kernel,
        in_specs=[whole] * 4,
        out_specs=[whole] * 2,
        out_shape=[
            jax.ShapeDtypeStruct((groups, 16, slots), f32),
            jax.ShapeDtypeStruct((groups, 8, slots), f32),
        ],
        compiler_params=pltpu.CompilerParams(vmem_limit_bytes=48 << 20),
    )(rank, own, moved, table)


def finish_kernel(member_ref, sums_ref, own_ref, slot_ref, pos_ref, vort_ref):
    member = member_ref[0]
    total = sums_ref[0]
    for sender in range(1, sums_ref.shape[0]):
        total = total + sums_ref[sender]
    width = own_ref.shape[2]
    for at, ref in ((0, own_ref), (1, slot_ref)):
        table = ref[member]
        result = (table + time_step * total[8 * at : 8 * at + 8]) * table[6:7]
        lanes = slice(at * width, at * width + width)
        pos_ref[0, 0, :, lanes] = result[0:3]
        vort_ref[0, 0, :, lanes] = result[3:6]


def finish(member, sums, own, slots):
    shape = jax.ShapeDtypeStruct((1, 1, 3, 2 * own.shape[2]), f32)
    return pl.pallas_call(
        finish_kernel,
        in_specs=[pl.BlockSpec(memory_space=pltpu.SMEM), whole, whole, whole],
        out_specs=[whole] * 2,
        out_shape=[shape, shape],
    )(member.reshape(1), sums, own, slots)


CHUNK = 128
FINE = 32
SLOTS = 6
AHEAD = 3


def pairs_kernel(sets, moved, copies, counted, *refs):
    refs = list(refs)
    count_ref = refs.pop(0) if counted else None
    tgt_ref = refs.pop(0)
    moved_ref = refs.pop(0) if moved else None
    source_refs = [refs.pop(0) for _ in range(3 * sets)]
    out_ref = refs.pop(0)
    table_ref = refs.pop(0) if moved else None
    tgt, near_sums, grad_sums = refs[:3]
    held = refs[3:]
    halves, rows, half = tgt_ref.shape

    def run():
        def joined(ref):
            return jnp.concatenate([ref[0], ref[1]], axis=1)

        table = joined(tgt_ref)
        if moved:
            step = joined(moved_ref.at[0])
            for sender in range(1, moved_ref.shape[0]):
                step = step + joined(moved_ref.at[sender])
            table = table + time_step * step
            table_ref[0] = table[:, :half]
            table_ref[1] = table[:, half:]
        where = [(table[k : k + 1, :] - centre) * (1.0 / unit) for k in range(3)]
        vortex = [table[3 + k : 4 + k, :] for k in range(3)]
        square = where[0] * where[0] + where[1] * where[1] + where[2] * where[2]
        square_parts = three_pieces(square)
        tgt[...] = jnp.zeros_like(tgt)
        for k in range(3):
            parts = three_pieces(-2.0 * where[k])
            for place, part in enumerate((0, 1, 0, 2, 0, 1)):
                tgt[3 * place + k : 3 * place + k + 1, :] = parts[part]
            tgt[18 + k : 19 + k, :] = jnp.ones_like(square)
            tgt[21 + k : 22 + k, :] = square_parts[k]
        targets = tgt[...].astype(bf16)
        near_sums[...] = jnp.zeros_like(near_sums)
        grad_sums[...] = jnp.zeros_like(grad_sums)
        start = jnp.minimum(pl.program_id(0), 0)
        per_set = source_refs[0].shape[1] // CHUNK
        chunks = sets * per_set

        def source(which, chunk):
            number, place = divmod(chunk, per_set)
            return source_refs[3 * number + which][:, place * CHUNK : (place + 1) * CHUNK]

        def read(ref, at, count):
            return ref[pl.ds(pl.multiple_of(start * CHUNK + at, count), count), :]

        def distances(chunk):
            held[chunk % SLOTS][...] = lax.dot_general(
                source(2, chunk), targets, (((0,), (0,)), ((), ())), preferred_element_type=f32
            )

        def weights(chunk):
            distance_ref = held[chunk % SLOTS]
            near_ref = held[SLOTS + chunk % SLOTS]
            grad_ref = held[2 * SLOTS + chunk % SLOTS]
            for at in range(0, CHUNK, FINE):
                root = lax.rsqrt(read(distance_ref, at, FINE))
                square_inv = root * root
                third = square_inv * root
                fifth = third * square_inv
                for ref, weight in (
                    (near_ref, third + fifth),
                    (grad_ref, fifth * (square_inv + 0.6)),
                ):
                    high = weight.astype(bf16)
                    ref[at : at + FINE, :] = high
                    ref[CHUNK + at : CHUNK + at + FINE, :] = (weight - high.astype(f32)).astype(bf16)

        def sums(chunk):
            for which, ref, total in ((0, held[SLOTS + chunk % SLOTS], near_sums), (1, held[2 * SLOTS + chunk % SLOTS], grad_sums)):
                terms = source(which, chunk)
                total[...] += dot(
                    jnp.concatenate([terms, terms], axis=1), read(ref, 0, 2 * CHUNK)
                )

        for chunk in range(AHEAD):
            distances(chunk)
        for chunk in range(chunks):
            if chunk + AHEAD < chunks:
                distances(chunk + AHEAD)
            if chunk >= AHEAD:
                sums(chunk - AHEAD)
            weights(chunk)
        for chunk in range(chunks - AHEAD, chunks):
            sums(chunk)
        near = near_sums[0:8, :] + near_sums[8:16, :] + near_sums[16:24, :]
        grad = grad_sums[0:24, :] + grad_sums[24:48, :] + grad_sums[48:72, :]

        def three(values, first):
            return [values[first + k : first + k + 1, :] for k in range(3)]

        near_vort, near_curl = three(near, 0), three(near, 3)
        grad_vort, grad_curl = three(grad, 0), three(grad, 3)
        turned = cross(where, near_vort)
        velocity = [velocity_factor * (turned[k] - near_curl[k]) for k in range(3)]
        along = vortex[0] * where[0] + vortex[1] * where[1] + vortex[2] * where[2]
        turned = cross(where, grad_vort)
        inner = [along * (turned[k] - grad_curl[k]) for k in range(3)]
        for axis in range(3):
            turned = cross(where, three(grad, 6 + 3 * axis))
            outer = three(grad, 15 + 3 * axis)
            inner = [inner[k] - vortex[axis] * (turned[k] - outer[k]) for k in range(3)]
        turned = cross(vortex, near_vort)
        stretch = [stretch_factor * (turned[k] - 5.0 * inner[k]) for k in range(3)]
        blank = jnp.zeros((2, 2 * half), f32)
        result = jnp.concatenate(velocity + stretch + [blank], axis=0)
        for copy in range(copies):
            out_ref[copy, 0] = result[:, :half]
            out_ref[copy, 1] = result[:, half:]

    if not counted:
        run()
        return
    used = pl.program_id(0) * 2 * half < count_ref[0, 0]
    pl.when(used)(run)

    @pl.when(jnp.logical_not(used))
    def _():
        out_ref[...] = jnp.zeros_like(out_ref)
        if moved:
            table_ref[...] = jnp.zeros_like(table_ref)


def pair_sums(table, source_sets, copies, moved=None, count=None):
    tiles, _, width = table.shape
    rows = 8
    pair = pl.BlockSpec((2, rows, width), lambda i: (i, 0, 0))
    operands, in_specs = [], []
    if count is not None:
        operands.append(count)
        in_specs.append(pl.BlockSpec(memory_space=pltpu.SMEM))
    operands.append(table)
    in_specs.append(pair)
    if moved is not None:
        operands.append(moved)
        in_specs.append(pl.BlockSpec((moved.shape[0], 2, rows, width), lambda i: (0, i, 0, 0)))
    sources = 0
    for source_set in source_sets:
        operands.extend(source_set)
        in_specs.extend([whole] * 3)
        sources += source_set[0].shape[1]
    out_shape = [jax.ShapeDtypeStruct((copies, tiles, rows, width), f32)]
    out_specs = [pl.BlockSpec((copies, 2, rows, width), lambda i: (0, i, 0, 0))]
    if moved is not None:
        out_shape.append(jax.ShapeDtypeStruct((tiles, rows, width), f32))
        out_specs.append(pair)
    pairs = sources * tiles * width
    return pl.pallas_call(
        functools.partial(pairs_kernel, len(source_sets), moved is not None, copies, count is not None),
        grid=(tiles // 2,),
        in_specs=in_specs,
        out_specs=out_specs,
        out_shape=out_shape,
        scratch_shapes=[
            pltpu.VMEM((32, 2 * width), f32),
            pltpu.VMEM((32, 2 * width), f32),
            pltpu.VMEM((80, 2 * width), f32),
        ]
        + [pltpu.VMEM((CHUNK, 2 * width), f32)] * SLOTS
        + [pltpu.VMEM((2 * CHUNK, 2 * width), bf16)] * (2 * SLOTS),
        compiler_params=pltpu.CompilerParams(vmem_limit_bytes=48 << 20),
        cost_estimate=pl.CostEstimate(
            flops=600 * pairs, bytes_accessed=300 * sources, transcendentals=pairs
        ),
    )(*operands)


def swap(values):
    return lax.all_to_all(values, "grp", split_axis=0, concat_axis=0, tiled=True)


def spread(values, groups):
    return swap(jnp.broadcast_to(values[None], (groups,) + values.shape))


def per_device(
    src_pos, src_vort, face_valid, tgt_pos, tgt_vort, mig_pos, mig_vort, mig_valid, mig_route
):
    groups = lax.axis_size("grp")
    slabs = lax.axis_size("slab")
    places = src_pos[0, 0]
    vortex = src_vort[0, 0]
    sources = places.shape[1]
    faces = face_valid.shape[3]
    own = tgt_pos.shape[3]
    slots = groups * CAP
    mine = jnp.concatenate(
        [tgt_pos[0, 0], tgt_vort[0, 0], jnp.ones((1, own), f32), jnp.zeros((1, own), f32)], axis=0
    )
    going_up, going_down = make_sends(
        places, vortex, face_valid[0, 0], mig_pos[0, 0], mig_vort[0, 0], mig_valid[0], mig_route[0, 0],
        2 * groups,
    )
    from_lower = lax.ppermute(going_up, "slab", [(i, (i + 1) % slabs) for i in range(slabs)])
    from_upper = lax.ppermute(going_down, "slab", [((i + 1) % slabs, i) for i in range(slabs)])
    own_set = prepare(sources, places, vortex)
    arrived = jnp.concatenate(
        [from_lower[:, faces + slots :], from_upper[:, faces : faces + slots]], axis=1
    )
    received = spread(jnp.concatenate([mine, arrived], axis=0), groups)
    face_set = prepare(2 * faces, from_lower, from_upper)
    sets = [own_set, face_set]
    (first_a,) = pair_sums(received, sets, groups)
    moved_a = swap(first_a.reshape(groups, -1, 128)).reshape(first_a.shape)
    table_b, rank, count = compact(received)
    (first_b,) = pair_sums(table_b, sets, groups, count=count)
    moved_b = swap(first_b.reshape(groups, -1, 128)).reshape(first_b.shape)
    second_a, table_a = pair_sums(received, sets, 1, moved=moved_a)
    second_b, table_b = pair_sums(table_b, sets, 1, moved=moved_b, count=count)
    rank = rank.reshape(2, groups, CAP, groups).transpose(0, 3, 2, 1).reshape(rank.shape)
    sums, table_b = expand_slots(rank, second_a[0], second_b[0], table_b)
    return finish(lax.axis_index("grp"), swap(sums), table_a, table_b)


def solution(mesh):
    return jax.shard_map(
        per_device,
        mesh=mesh,
        in_specs=(
            P("slab", "grp", None, None),
            P("slab", "grp", None, None),
            P("slab", "grp", None, None),
            P("slab", "grp", None, None),
            P("slab", "grp", None, None),
            P("slab", "grp", None, None),
            P("slab", "grp", None, None),
            P("slab", "grp", None),
            P("slab", "grp", None, None),
        ),
        out_specs=(P("slab", "grp", None, None), P("slab", "grp", None, None)),
        check_vma=False,
    )
```

```python
import functools
import math

import jax
import jax.numpy as jnp
from jax import lax
from jax.experimental import pallas as pl
from jax.experimental.pallas import tpu as pltpu
from jax.sharding import PartitionSpec as P

CAP = 8
STEPS = 2
core_square = 0.0225
time_step = 0.1
strength = 0.03 / (4.0 * math.pi)

centre = 0.5
unit_square = 1.5 * core_square
unit = math.sqrt(unit_square)
velocity_factor = -strength / unit_square
stretch_factor = -strength / (unit_square * unit)
f32 = jnp.float32
bf16 = jnp.bfloat16
whole = pl.BlockSpec(memory_space=pltpu.VMEM)


def three_pieces(values):
    high = values.astype(bf16).astype(f32)
    rest = values - high
    middle = rest.astype(bf16).astype(f32)
    low = rest - middle
    return high, middle, low


def two_pieces(values):
    high = values.astype(bf16)
    low = (values - high.astype(f32)).astype(bf16)
    return jnp.concatenate([high, low], axis=0)


def dot(left, right):
    return lax.dot_general(left, right, (((1,), (0,)), ((), ())), preferred_element_type=f32)


def cross(left, right):
    return [
        left[(k + 1) % 3] * right[(k + 2) % 3] - left[(k + 2) % 3] * right[(k + 1) % 3]
        for k in range(3)
    ]


def send_kernel(
    faces, pos_ref, vort_ref, valid_ref, mig_pos_ref, mig_vort_ref, mig_valid_ref, route_ref,
    up_ref, down_ref, record,
):
    sources = pos_ref.shape[1]
    migrants = route_ref.shape[0]
    slots = (up_ref.shape[1] - faces) // 2
    destinations = 2 * slots // CAP
    route = route_ref[...]
    matches = route == lax.broadcasted_iota(jnp.int32, (migrants, destinations), 1)
    matches = jnp.where(matches, 1.0, 0.0)
    earlier = lax.broadcasted_iota(jnp.int32, (migrants, migrants), 0) > lax.broadcasted_iota(
        jnp.int32, (migrants, migrants), 1
    )
    before = dot(jnp.where(earlier, 1.0, 0.0).astype(bf16), matches.astype(bf16))
    order = jnp.sum(before * matches, axis=1, keepdims=True).astype(jnp.int32)
    placing = (route * CAP + order) == lax.broadcasted_iota(jnp.int32, (migrants, 2 * slots), 1)
    placing = jnp.where(placing, 1.0, 0.0).astype(bf16)
    record[...] = jnp.zeros_like(record)
    record[0:3, :] = mig_pos_ref[...]
    record[3:6, :] = mig_vort_ref[...]
    record[6:7, :] = mig_valid_ref[...].astype(f32)
    pieces = jnp.concatenate(three_pieces(record[...]), axis=0)
    placed = dot(jnp.concatenate([pieces, jnp.zeros((8, migrants), f32)], axis=0).astype(bf16), placing)
    placed = placed[0:8] + placed[8:16] + placed[16:24]
    first = lax.broadcasted_iota(jnp.int32, placed.shape, 0) == 0
    for ref, begin, shift, which in ((down_ref, 0, 1.0, 0), (up_ref, sources - faces, -1.0, 1)):
        piece = slice(begin, begin + faces)
        mask = valid_ref[which : which + 1, :].astype(f32)
        ref[0:1, :faces] = pos_ref[0:1, piece] + shift
        ref[1:3, :faces] = pos_ref[1:3, piece]
        ref[3:6, :faces] = vort_ref[:, piece] * mask
        ref[6:8, :faces] = jnp.zeros((2, faces), f32)
        ref[:, faces:] = jnp.where(first, placed + shift, placed)


def make_sends(places, vortex, valid, mig_pos, mig_vort, mig_valid, route, destinations):
    faces = valid.shape[1]
    shape = jax.ShapeDtypeStruct((8, faces + destinations * CAP), f32)
    return pl.pallas_call(
        functools.partial(send_kernel, faces),
        in_specs=[whole] * 7,
        out_specs=[whole] * 2,
        out_shape=[shape, shape],
        scratch_shapes=[pltpu.VMEM((8, route.shape[0]), f32)],
        compiler_params=pltpu.CompilerParams(vmem_limit_bytes=48 << 20),
    )(places, vortex, valid, mig_pos, mig_vort, mig_valid, route)


def prepare_kernel(length, *refs):
    source_refs = refs[:-5]
    near_ref, grad_ref, dist_ref, rows, dist = refs[-5:]

    def columns(row):
        if source_refs[0].shape[0] == 3:
            return source_refs[row // 3][row % 3 : row % 3 + 1, :]
        return jnp.concatenate([ref[row : row + 1, : length // 2] for ref in source_refs], axis=1)

    places = [(columns(k) - centre) * (1.0 / unit) for k in range(3)]
    vortex = [columns(3 + k) for k in range(3)]
    curled = cross(places, vortex)
    for k in range(3):
        rows[k : k + 1, :] = vortex[k]
        rows[3 + k : 4 + k, :] = curled[k]
        for l in range(3):
            at = 6 + 3 * k + l
            rows[at : at + 1, :] = places[k] * vortex[l]
            rows[at + 9 : at + 10, :] = places[k] * curled[l]
    high, middle, low = three_pieces(rows[...])
    blank = jnp.zeros((8, high.shape[1]), f32)
    grad_ref[...] = jnp.concatenate([high, middle, low, blank], axis=0).astype(bf16)
    near_ref[...] = jnp.concatenate([high[0:8], middle[0:8], low[0:8], blank], axis=0).astype(bf16)
    square = places[0] * places[0] + places[1] * places[1] + places[2] * places[2]
    square_parts = three_pieces(square + core_square / unit_square)
    dist[...] = jnp.zeros_like(dist)
    for k in range(3):
        parts = three_pieces(places[k])
        for place, part in enumerate((0, 0, 1, 0, 2, 1)):
            dist[3 * place + k : 3 * place + k + 1, :] = parts[part]
        dist[18 + k : 19 + k, :] = square_parts[k]
        dist[21 + k : 22 + k, :] = jnp.ones_like(square)
    dist_ref[...] = dist[...].astype(bf16)


def prepare(length, *sources):
    return pl.pallas_call(
        functools.partial(prepare_kernel, length),
        in_specs=[whole] * len(sources),
        out_specs=[whole] * 3,
        out_shape=[
            jax.ShapeDtypeStruct((32, length), bf16),
            jax.ShapeDtypeStruct((80, length), bf16),
            jax.ShapeDtypeStruct((32, length), bf16),
        ],
        scratch_shapes=[pltpu.VMEM((24, length), f32), pltpu.VMEM((32, length), f32)],
        compiler_params=pltpu.CompilerParams(vmem_limit_bytes=48 << 20),
    )(*sources)


def compact_kernel(arrived_ref, table_ref, rank_ref, count_ref):
    groups, _, slots = arrived_ref.shape
    valid = jnp.concatenate([arrived_ref[m, 14:15, :] for m in range(groups)], axis=0)
    row = lax.broadcasted_iota(jnp.int32, (slots, slots), 0)
    column = lax.broadcasted_iota(jnp.int32, (slots, slots), 1)
    earlier = jnp.where(row < column, 1.0, 0.0).astype(bf16)
    same = jnp.where(row == column, 1.0, 0.0).astype(bf16)

    def turned(matrix, which):
        return lax.dot_general(
            matrix, which, (((0,), (1,)), ((), ())), preferred_element_type=f32
        )

    flags = valid.astype(bf16)
    within = turned(earlier, flags)
    living = turned(same, flags)
    totals = jnp.sum(living, axis=0, keepdims=True)
    ahead = [jnp.zeros((1, 1), f32)]
    for m in range(1, groups):
        ahead.append(ahead[-1] + totals[:, m - 1 : m])
    rank = jnp.where(living > 0.5, within + jnp.concatenate(ahead, axis=1), -1.0)
    rank_ref[...] = rank
    count_ref[0, 0] = jnp.sum(valid).astype(jnp.int32)
    wanted = lax.broadcasted_iota(jnp.int32, (slots, groups * slots), 1).astype(f32)
    placed = jnp.zeros((32, groups * slots), f32)
    for m in range(groups):
        pieces = three_pieces(arrived_ref[m, 8:16, :])
        pieces = jnp.concatenate(pieces + (jnp.zeros((8, slots), f32),), axis=0).astype(bf16)
        chosen = jnp.where(rank[:, m : m + 1] == wanted, 1.0, 0.0).astype(bf16)
        placed = placed + dot(pieces, chosen)
    placed = placed[0:8] + placed[8:16] + placed[16:24]
    for m in range(groups):
        table_ref[m] = placed[:, m * slots : (m + 1) * slots]


def compact(received):
    groups, _, slots = received.shape
    return pl.pallas_call(
        compact_kernel,
        in_specs=[whole],
        out_specs=[whole, whole, pl.BlockSpec(memory_space=pltpu.SMEM)],
        out_shape=[
            jax.ShapeDtypeStruct((groups, 8, slots), f32),
            jax.ShapeDtypeStruct((slots, groups), f32),
            jax.ShapeDtypeStruct((1, 1), jnp.int32),
        ],
        compiler_params=pltpu.CompilerParams(vmem_limit_bytes=48 << 20),
    )(received)


def expand_kernel(rank_ref, own_ref, moved_ref, table_ref, sums_ref, places_ref):
    groups, _, slots = moved_ref.shape
    rows = [
        jnp.concatenate([ref[m] for m in range(groups)], axis=1) for ref in (moved_ref, table_ref)
    ]
    pieces = jnp.concatenate(three_pieces(jnp.concatenate(rows, axis=0)), axis=0).astype(bf16)
    wanted = lax.broadcasted_iota(jnp.int32, (slots, groups * slots), 1).astype(f32)
    for member in range(groups):
        chosen = jnp.where(rank_ref[:, member : member + 1] == wanted, 1.0, 0.0).astype(bf16)
        found = lax.dot_general(
            pieces, chosen, (((1,), (1,)), ((), ())), preferred_element_type=f32
        )
        found = found[0:16] + found[16:32] + found[32:48]
        sums_ref[member, 0:8, :] = own_ref[member]
        sums_ref[member, 8:16, :] = found[0:8]
        places_ref[member] = found[8:16]


def expand_slots(rank, own, moved, table):
    groups, _, slots = moved.shape
    return pl.pallas_call(
        expand_kernel,
        in_specs=[whole] * 4,
        out_specs=[whole] * 2,
        out_shape=[
            jax.ShapeDtypeStruct((groups, 16, slots), f32),
            jax.ShapeDtypeStruct((groups, 8, slots), f32),
        ],
        compiler_params=pltpu.CompilerParams(vmem_limit_bytes=48 << 20),
    )(rank, own, moved, table)


CHUNK = 128
FINE = 16
SLOTS = 6
AHEAD = 3


def pairs_kernel(sets, moved, copies, counted, *refs):
    refs = list(refs)
    count_ref = refs.pop(0) if counted else None
    tgt_ref = refs.pop(0)
    moved_ref = refs.pop(0) if moved else None
    source_refs = [refs.pop(0) for _ in range(3 * sets)]
    out_ref = refs.pop(0)
    table_ref = refs.pop(0) if moved else None
    tgt, near_sums, grad_sums = refs[:3]
    held = refs[3:]
    halves, rows, half = tgt_ref.shape

    def run(parts):
        lanes = parts * half

        def joined(ref):
            return ref[0] if parts == 1 else jnp.concatenate([ref[0], ref[1]], axis=1)

        def store(ref, values):
            for part in range(halves):
                at = slice(part * half, part * half + half)
                ref[part] = values[:, at] if part < parts else jnp.zeros((rows, half), f32)

        table = joined(tgt_ref)
        if moved:
            step = joined(moved_ref.at[0])
            for sender in range(1, moved_ref.shape[0]):
                step = step + joined(moved_ref.at[sender])
            table = table + time_step * step
            store(table_ref, table)
        where = [(table[k : k + 1, :] - centre) * (1.0 / unit) for k in range(3)]
        vortex = [table[3 + k : 4 + k, :] for k in range(3)]
        square = where[0] * where[0] + where[1] * where[1] + where[2] * where[2]
        square_parts = three_pieces(square)
        tgt[...] = jnp.zeros_like(tgt)
        for k in range(3):
            pieces = three_pieces(-2.0 * where[k])
            for place, piece in enumerate((0, 1, 0, 2, 0, 1)):
                tgt[3 * place + k : 3 * place + k + 1, :lanes] = pieces[piece]
            tgt[18 + k : 19 + k, :lanes] = jnp.ones_like(square)
            tgt[21 + k : 22 + k, :lanes] = square_parts[k]
        targets = tgt[:, :lanes].astype(bf16)
        near_sums[...] = jnp.zeros_like(near_sums)
        grad_sums[...] = jnp.zeros_like(grad_sums)
        start = jnp.minimum(pl.program_id(0), 0)
        per_set = source_refs[0].shape[1] // CHUNK
        chunks = sets * per_set

        def source(which, chunk):
            number, place = divmod(chunk, per_set)
            return source_refs[3 * number + which][:, place * CHUNK : (place + 1) * CHUNK]

        def read(ref, at, count):
            return ref[pl.ds(pl.multiple_of(start * CHUNK + at, count), count), :lanes]

        def distances(chunk):
            held[chunk % SLOTS][:, :lanes] = lax.dot_general(
                source(2, chunk), targets, (((0,), (0,)), ((), ())), preferred_element_type=f32
            )

        def weights(chunk):
            distance_ref = held[chunk % SLOTS]
            near_ref = held[SLOTS + chunk % SLOTS]
            grad_ref = held[2 * SLOTS + chunk % SLOTS]
            for at in range(0, CHUNK, FINE):
                root = lax.rsqrt(read(distance_ref, at, FINE))
                square_inv = root * root
                third = square_inv * root
                fifth = third * square_inv
                for ref, weight in (
                    (near_ref, third + fifth),
                    (grad_ref, fifth * (square_inv + 0.6)),
                ):
                    high = weight.astype(bf16)
                    ref[at : at + FINE, :lanes] = high
                    low = (weight - high.astype(f32)).astype(bf16)
                    ref[CHUNK + at : CHUNK + at + FINE, :lanes] = low

        def sums(chunk):
            for which, total in ((0, near_sums), (1, grad_sums)):
                ref = held[(1 + which) * SLOTS + chunk % SLOTS]
                terms = source(which, chunk)
                total[:, :lanes] += dot(
                    jnp.concatenate([terms, terms], axis=1), read(ref, 0, 2 * CHUNK)
                )

        for chunk in range(AHEAD):
            distances(chunk)
        for chunk in range(chunks):
            if chunk + AHEAD < chunks:
                distances(chunk + AHEAD)
            if chunk >= AHEAD:
                sums(chunk - AHEAD)
            weights(chunk)
        for chunk in range(chunks - AHEAD, chunks):
            sums(chunk)
        near = near_sums[0:8, :lanes] + near_sums[8:16, :lanes] + near_sums[16:24, :lanes]
        grad = grad_sums[0:24, :lanes] + grad_sums[24:48, :lanes] + grad_sums[48:72, :lanes]

        def three(values, first):
            return [values[first + k : first + k + 1, :] for k in range(3)]

        near_vort, near_curl = three(near, 0), three(near, 3)
        grad_vort, grad_curl = three(grad, 0), three(grad, 3)
        turned = cross(where, near_vort)
        velocity = [velocity_factor * (turned[k] - near_curl[k]) for k in range(3)]
        along = vortex[0] * where[0] + vortex[1] * where[1] + vortex[2] * where[2]
        turned = cross(where, grad_vort)
        inner = [along * (turned[k] - grad_curl[k]) for k in range(3)]
        for axis in range(3):
            turned = cross(where, three(grad, 6 + 3 * axis))
            outer = three(grad, 15 + 3 * axis)
            inner = [inner[k] - vortex[axis] * (turned[k] - outer[k]) for k in range(3)]
        turned = cross(vortex, near_vort)
        stretch = [stretch_factor * (turned[k] - 5.0 * inner[k]) for k in range(3)]
        blank = jnp.zeros((2, lanes), f32)
        result = jnp.concatenate(velocity + stretch + [blank], axis=0)
        for copy in range(copies):
            store(out_ref.at[copy], result)

    if not counted:
        run(halves)
        return
    left = count_ref[0, 0] - pl.program_id(0) * halves * half
    pl.when(left > half)(functools.partial(run, halves))
    pl.when(jnp.logical_and(left > 0, left <= half))(functools.partial(run, 1))

    @pl.when(left <= 0)
    def _():
        out_ref[...] = jnp.zeros_like(out_ref)
        if moved:
            table_ref[...] = jnp.zeros_like(table_ref)


def pair_sums(table, source_sets, copies, moved=None, count=None):
    tiles, _, width = table.shape
    rows = 8
    pair = pl.BlockSpec((2, rows, width), lambda i: (i, 0, 0))
    operands, in_specs = [], []
    if count is not None:
        operands.append(count)
        in_specs.append(pl.BlockSpec(memory_space=pltpu.SMEM))
    operands.append(table)
    in_specs.append(pair)
    if moved is not None:
        operands.append(moved)
        in_specs.append(pl.BlockSpec((moved.shape[0], 2, rows, width), lambda i: (0, i, 0, 0)))
    sources = 0
    for source_set in source_sets:
        operands.extend(source_set)
        in_specs.extend([whole] * 3)
        sources += source_set[0].shape[1]
    out_shape = [jax.ShapeDtypeStruct((copies, tiles, rows, width), f32)]
    out_specs = [pl.BlockSpec((copies, 2, rows, width), lambda i: (0, i, 0, 0))]
    if moved is not None:
        out_shape.append(jax.ShapeDtypeStruct((tiles, rows, width), f32))
        out_specs.append(pair)
    pairs = sources * tiles * width
    return pl.pallas_call(
        functools.partial(pairs_kernel, len(source_sets), moved is not None, copies, count is not None),
        grid=(tiles // 2,),
        in_specs=in_specs,
        out_specs=out_specs,
        out_shape=out_shape,
        scratch_shapes=[
            pltpu.VMEM((32, 2 * width), f32),
            pltpu.VMEM((32, 2 * width), f32),
            pltpu.VMEM((80, 2 * width), f32),
        ]
        + [pltpu.VMEM((CHUNK, 2 * width), f32)] * SLOTS
        + [pltpu.VMEM((2 * CHUNK, 2 * width), bf16)] * (2 * SLOTS),
        compiler_params=pltpu.CompilerParams(vmem_limit_bytes=48 << 20),
        cost_estimate=pl.CostEstimate(
            flops=600 * pairs, bytes_accessed=300 * sources, transcendentals=pairs
        ),
    )(*operands)


def swap(values):
    return lax.all_to_all(values, "grp", split_axis=0, concat_axis=0, tiled=True)


def spread(values, groups):
    return swap(jnp.broadcast_to(values[None], (groups,) + values.shape))


def per_device(
    src_pos, src_vort, face_valid, tgt_pos, tgt_vort, mig_pos, mig_vort, mig_valid, mig_route
):
    groups = lax.axis_size("grp")
    slabs = lax.axis_size("slab")
    places = src_pos[0, 0]
    vortex = src_vort[0, 0]
    sources = places.shape[1]
    faces = face_valid.shape[3]
    own = tgt_pos.shape[3]
    slots = groups * CAP
    mine = jnp.concatenate(
        [tgt_pos[0, 0], tgt_vort[0, 0], jnp.ones((1, own), f32), jnp.zeros((1, own), f32)], axis=0
    )
    going_up, going_down = make_sends(
        places, vortex, face_valid[0, 0], mig_pos[0, 0], mig_vort[0, 0], mig_valid[0], mig_route[0, 0],
        2 * groups,
    )
    from_lower = lax.ppermute(going_up, "slab", [(i, (i + 1) % slabs) for i in range(slabs)])
    from_upper = lax.ppermute(going_down, "slab", [((i + 1) % slabs, i) for i in range(slabs)])
    own_set = prepare(sources, places, vortex)
    arrived = jnp.concatenate(
        [from_lower[:, faces + slots :], from_upper[:, faces : faces + slots]], axis=1
    )
    received = spread(jnp.concatenate([mine, arrived], axis=0), groups)
    face_set = prepare(2 * faces, from_lower, from_upper)
    sets = [own_set, face_set]
    (first_a,) = pair_sums(received, sets, groups)
    moved_a = swap(first_a.reshape(groups, -1, 128)).reshape(first_a.shape)
    table_b, rank, count = compact(received)
    (first_b,) = pair_sums(table_b, sets, groups, count=count)
    moved_b = swap(first_b.reshape(groups, -1, 128)).reshape(first_b.shape)
    second_a, table_a = pair_sums(received, sets, 1, moved=moved_a)
    second_b, table_b = pair_sums(table_b, sets, 1, moved=moved_b, count=count)
    rank = rank.reshape(2, groups, CAP, groups).transpose(0, 3, 2, 1).reshape(rank.shape)
    sums, table_b = expand_slots(rank, second_a[0], second_b[0], table_b)
    sums = swap(sums)
    member = lax.axis_index("grp")
    own = [lax.dynamic_index_in_dim(t, member, 0, keepdims=False) for t in (table_a, table_b)]
    total = jnp.sum(sums, axis=0)
    outs = []
    for first in (0, 3):
        moved = [
            (own[k][first : first + 3] + time_step * total[8 * k + first : 8 * k + first + 3])
            * own[k][6:7]
            for k in range(2)
        ]
        outs.append(jnp.concatenate(moved, axis=1)[None, None])
    return tuple(outs)


def solution(mesh):
    return jax.shard_map(
        per_device,
        mesh=mesh,
        in_specs=(
            P("slab", "grp", None, None),
            P("slab", "grp", None, None),
            P("slab", "grp", None, None),
            P("slab", "grp", None, None),
            P("slab", "grp", None, None),
            P("slab", "grp", None, None),
            P("slab", "grp", None, None),
            P("slab", "grp", None),
            P("slab", "grp", None, None),
        ),
        out_specs=(P("slab", "grp", None, None), P("slab", "grp", None, None)),
        check_vma=False,
    )
```

```python
import functools
import math

import jax
import jax.numpy as jnp
from jax import lax
from jax.experimental import pallas as pl
from jax.experimental.pallas import tpu as pltpu
from jax.sharding import PartitionSpec as P

CAP = 8
STEPS = 2
core_square = 0.0225
time_step = 0.1
strength = 0.03 / (4.0 * math.pi)

centre = 0.5
unit_square = 1.5 * core_square
unit = math.sqrt(unit_square)
velocity_factor = -strength / unit_square
stretch_factor = -strength / (unit_square * unit)
f32 = jnp.float32
bf16 = jnp.bfloat16
whole = pl.BlockSpec(memory_space=pltpu.VMEM)


def three_pieces(values):
    high = values.astype(bf16).astype(f32)
    rest = values - high
    middle = rest.astype(bf16).astype(f32)
    low = rest - middle
    return high, middle, low


def two_pieces(values):
    high = values.astype(bf16)
    low = (values - high.astype(f32)).astype(bf16)
    return jnp.concatenate([high, low], axis=0)


def dot(left, right):
    return lax.dot_general(left, right, (((1,), (0,)), ((), ())), preferred_element_type=f32)


def cross(left, right):
    return [
        left[(k + 1) % 3] * right[(k + 2) % 3] - left[(k + 2) % 3] * right[(k + 1) % 3]
        for k in range(3)
    ]


def send_kernel(
    faces, pos_ref, vort_ref, valid_ref, mig_pos_ref, mig_vort_ref, mig_valid_ref, route_ref,
    up_ref, down_ref, record,
):
    sources = pos_ref.shape[2]
    migrants = route_ref.shape[0]
    slots = (up_ref.shape[1] - faces) // 2
    destinations = 2 * slots // CAP
    route = route_ref[...]
    matches = route == lax.broadcasted_iota(jnp.int32, (migrants, destinations), 1)
    matches = jnp.where(matches, 1.0, 0.0)
    earlier = lax.broadcasted_iota(jnp.int32, (migrants, migrants), 0) > lax.broadcasted_iota(
        jnp.int32, (migrants, migrants), 1
    )
    before = dot(jnp.where(earlier, 1.0, 0.0).astype(bf16), matches.astype(bf16))
    order = jnp.sum(before * matches, axis=1, keepdims=True).astype(jnp.int32)
    placing = (route * CAP + order) == lax.broadcasted_iota(jnp.int32, (migrants, 2 * slots), 1)
    placing = jnp.where(placing, 1.0, 0.0).astype(bf16)
    record[...] = jnp.zeros_like(record)
    for k in range(3):
        record[k : k + 1, :] = mig_pos_ref[k]
        record[3 + k : 4 + k, :] = mig_vort_ref[k]
    record[6:7, :] = mig_valid_ref[...].astype(f32)
    pieces = jnp.concatenate(three_pieces(record[...]), axis=0)
    placed = dot(jnp.concatenate([pieces, jnp.zeros((8, migrants), f32)], axis=0).astype(bf16), placing)
    placed = placed[0:8] + placed[8:16] + placed[16:24]
    first = lax.broadcasted_iota(jnp.int32, placed.shape, 0) == 0
    for ref, begin, shift, which in ((down_ref, 0, 1.0, 0), (up_ref, sources - faces, -1.0, 1)):
        piece = slice(begin, begin + faces)
        mask = valid_ref[which : which + 1, :].astype(f32)
        for k in range(3):
            place = pos_ref[k, :, piece]
            ref[k : k + 1, :faces] = place + shift if k == 0 else place
            ref[3 + k : 4 + k, :faces] = vort_ref[k, :, piece] * mask
        ref[6:8, :faces] = jnp.zeros((2, faces), f32)
        ref[:, faces:] = jnp.where(first, placed + shift, placed)


def make_sends(places, vortex, valid, mig_pos, mig_vort, mig_valid, route, destinations):
    faces = valid.shape[1]
    shape = jax.ShapeDtypeStruct((8, faces + destinations * CAP), f32)
    return pl.pallas_call(
        functools.partial(send_kernel, faces),
        in_specs=[whole] * 7,
        out_specs=[whole] * 2,
        out_shape=[shape, shape],
        scratch_shapes=[pltpu.VMEM((8, route.shape[0]), f32)],
        compiler_params=pltpu.CompilerParams(vmem_limit_bytes=48 << 20),
    )(places, vortex, valid, mig_pos, mig_vort, mig_valid, route)


def prepare_kernel(length, *refs):
    source_refs = refs[:-5]
    near_ref, grad_ref, dist_ref, rows, dist = refs[-5:]

    def columns(row):
        if source_refs[0].shape[0] == 3:
            return source_refs[row // 3][row % 3]
        return jnp.concatenate([ref[row : row + 1, : length // 2] for ref in source_refs], axis=1)

    places = [(columns(k) - centre) * (1.0 / unit) for k in range(3)]
    vortex = [columns(3 + k) for k in range(3)]
    curled = cross(places, vortex)
    for k in range(3):
        rows[k : k + 1, :] = vortex[k]
        rows[3 + k : 4 + k, :] = curled[k]
        for l in range(3):
            at = 6 + 3 * k + l
            rows[at : at + 1, :] = places[k] * vortex[l]
            rows[at + 9 : at + 10, :] = places[k] * curled[l]
    high, middle, low = three_pieces(rows[...])
    blank = jnp.zeros((8, high.shape[1]), f32)
    grad_ref[...] = jnp.concatenate([high, middle, low, blank], axis=0).astype(bf16)
    near_ref[...] = jnp.concatenate([high[0:8], middle[0:8], low[0:8], blank], axis=0).astype(bf16)
    square = places[0] * places[0] + places[1] * places[1] + places[2] * places[2]
    square_parts = three_pieces(square + core_square / unit_square)
    dist[...] = jnp.zeros_like(dist)
    for k in range(3):
        parts = three_pieces(places[k])
        for place, part in enumerate((0, 0, 1, 0, 2, 1)):
            dist[3 * place + k : 3 * place + k + 1, :] = parts[part]
        dist[18 + k : 19 + k, :] = square_parts[k]
        dist[21 + k : 22 + k, :] = jnp.ones_like(square)
    dist_ref[...] = dist[...].astype(bf16)


def prepare(length, *sources):
    return pl.pallas_call(
        functools.partial(prepare_kernel, length),
        in_specs=[whole] * len(sources),
        out_specs=[whole] * 3,
        out_shape=[
            jax.ShapeDtypeStruct((32, length), bf16),
            jax.ShapeDtypeStruct((80, length), bf16),
            jax.ShapeDtypeStruct((32, length), bf16),
        ],
        scratch_shapes=[pltpu.VMEM((24, length), f32), pltpu.VMEM((32, length), f32)],
        compiler_params=pltpu.CompilerParams(vmem_limit_bytes=48 << 20),
    )(*sources)


def compact_kernel(arrived_ref, table_ref, rank_ref, count_ref):
    groups, _, slots = arrived_ref.shape
    valid = jnp.concatenate([arrived_ref[m, 14:15, :] for m in range(groups)], axis=0)
    row = lax.broadcasted_iota(jnp.int32, (slots, slots), 0)
    column = lax.broadcasted_iota(jnp.int32, (slots, slots), 1)
    earlier = jnp.where(row < column, 1.0, 0.0).astype(bf16)
    same = jnp.where(row == column, 1.0, 0.0).astype(bf16)

    def turned(matrix, which):
        return lax.dot_general(
            matrix, which, (((0,), (1,)), ((), ())), preferred_element_type=f32
        )

    flags = valid.astype(bf16)
    within = turned(earlier, flags)
    living = turned(same, flags)
    totals = jnp.sum(living, axis=0, keepdims=True)
    ahead = [jnp.zeros((1, 1), f32)]
    for m in range(1, groups):
        ahead.append(ahead[-1] + totals[:, m - 1 : m])
    rank = jnp.where(living > 0.5, within + jnp.concatenate(ahead, axis=1), -1.0)
    rank_ref[...] = rank
    count_ref[0, 0] = jnp.sum(valid).astype(jnp.int32)
    wanted = lax.broadcasted_iota(jnp.int32, (slots, groups * slots), 1).astype(f32)
    placed = jnp.zeros((32, groups * slots), f32)
    for m in range(groups):
        pieces = three_pieces(arrived_ref[m, 8:16, :])
        pieces = jnp.concatenate(pieces + (jnp.zeros((8, slots), f32),), axis=0).astype(bf16)
        chosen = jnp.where(rank[:, m : m + 1] == wanted, 1.0, 0.0).astype(bf16)
        placed = placed + dot(pieces, chosen)
    placed = placed[0:8] + placed[8:16] + placed[16:24]
    for m in range(groups):
        table_ref[m] = placed[:, m * slots : (m + 1) * slots]


def compact(received):
    groups, _, slots = received.shape
    return pl.pallas_call(
        compact_kernel,
        in_specs=[whole],
        out_specs=[whole, whole, pl.BlockSpec(memory_space=pltpu.SMEM)],
        out_shape=[
            jax.ShapeDtypeStruct((groups, 8, slots), f32),
            jax.ShapeDtypeStruct((slots, groups), f32),
            jax.ShapeDtypeStruct((1, 1), jnp.int32),
        ],
        compiler_params=pltpu.CompilerParams(vmem_limit_bytes=48 << 20),
    )(received)


def expand_kernel(rank_ref, own_ref, moved_ref, table_ref, sums_ref, places_ref):
    groups, _, slots = moved_ref.shape
    rows = [
        jnp.concatenate([ref[m] for m in range(groups)], axis=1) for ref in (moved_ref, table_ref)
    ]
    pieces = jnp.concatenate(three_pieces(jnp.concatenate(rows, axis=0)), axis=0).astype(bf16)
    wanted = lax.broadcasted_iota(jnp.int32, (groups * slots, slots), 0).astype(f32)
    for member in range(groups):
        chosen = jnp.where(rank_ref[member : member + 1, :] == wanted, 1.0, 0.0).astype(bf16)
        found = dot(pieces, chosen)
        found = found[0:16] + found[16:32] + found[32:48]
        sums_ref[member, 0:8, :] = own_ref[member]
        sums_ref[member, 8:16, :] = found[0:8]
        places_ref[member] = found[8:16]


def expand_slots(rank, own, moved, table):
    groups, _, slots = moved.shape
    return pl.pallas_call(
        expand_kernel,
        in_specs=[whole] * 4,
        out_specs=[whole] * 2,
        out_shape=[
            jax.ShapeDtypeStruct((groups, 16, slots), f32),
            jax.ShapeDtypeStruct((groups, 8, slots), f32),
        ],
        compiler_params=pltpu.CompilerParams(vmem_limit_bytes=48 << 20),
    )(rank, own, moved, table)


CHUNK = 128
FINE = 16
SLOTS = 6
AHEAD = 3


def pairs_kernel(sets, moved, copies, counted, *refs):
    refs = list(refs)
    count_ref = refs.pop(0) if counted else None
    tgt_ref = refs.pop(0)
    moved_ref = refs.pop(0) if moved else None
    source_refs = [refs.pop(0) for _ in range(3 * sets)]
    out_ref = refs.pop(0)
    table_ref = refs.pop(0) if moved else None
    tgt, near_sums, grad_sums = refs[:3]
    held = refs[3:]
    halves, rows, half = tgt_ref.shape

    def run(parts):
        lanes = parts * half

        def joined(ref):
            return ref[0] if parts == 1 else jnp.concatenate([ref[0], ref[1]], axis=1)

        def store(ref, values):
            for part in range(halves):
                at = slice(part * half, part * half + half)
                ref[part] = values[:, at] if part < parts else jnp.zeros((rows, half), f32)

        table = joined(tgt_ref)
        if moved:
            step = joined(moved_ref.at[0])
            for sender in range(1, moved_ref.shape[0]):
                step = step + joined(moved_ref.at[sender])
            table = table + time_step * step
            store(table_ref, table)
        where = [(table[k : k + 1, :] - centre) * (1.0 / unit) for k in range(3)]
        vortex = [table[3 + k : 4 + k, :] for k in range(3)]
        square = where[0] * where[0] + where[1] * where[1] + where[2] * where[2]
        square_parts = three_pieces(square)
        tgt[...] = jnp.zeros_like(tgt)
        for k in range(3):
            pieces = three_pieces(-2.0 * where[k])
            for place, piece in enumerate((0, 1, 0, 2, 0, 1)):
                tgt[3 * place + k : 3 * place + k + 1, :lanes] = pieces[piece]
            tgt[18 + k : 19 + k, :lanes] = jnp.ones_like(square)
            tgt[21 + k : 22 + k, :lanes] = square_parts[k]
        targets = tgt[:, :lanes].astype(bf16)
        near_sums[...] = jnp.zeros_like(near_sums)
        grad_sums[...] = jnp.zeros_like(grad_sums)
        start = jnp.minimum(pl.program_id(0), 0)
        per_set = source_refs[0].shape[1] // CHUNK
        chunks = sets * per_set

        def source(which, chunk):
            number, place = divmod(chunk, per_set)
            return source_refs[3 * number + which][:, place * CHUNK : (place + 1) * CHUNK]

        def read(ref, at, count):
            return ref[pl.ds(pl.multiple_of(start * CHUNK + at, count), count), :lanes]

        def distances(chunk):
            held[chunk % SLOTS][:, :lanes] = lax.dot_general(
                source(2, chunk), targets, (((0,), (0,)), ((), ())), preferred_element_type=f32
            )

        def weights(chunk):
            distance_ref = held[chunk % SLOTS]
            near_ref = held[SLOTS + chunk % SLOTS]
            grad_ref = held[2 * SLOTS + chunk % SLOTS]
            for at in range(0, CHUNK, FINE):
                root = lax.rsqrt(read(distance_ref, at, FINE))
                square_inv = root * root
                third = square_inv * root
                fifth = third * square_inv
                for ref, weight in (
                    (near_ref, third + fifth),
                    (grad_ref, fifth * (square_inv + 0.6)),
                ):
                    high = weight.astype(bf16)
                    ref[at : at + FINE, :lanes] = high
                    low = (weight - high.astype(f32)).astype(bf16)
                    ref[CHUNK + at : CHUNK + at + FINE, :lanes] = low

        def sums(chunk):
            for which, total in ((0, near_sums), (1, grad_sums)):
                ref = held[(1 + which) * SLOTS + chunk % SLOTS]
                terms = source(which, chunk)
                total[:, :lanes] += dot(
                    jnp.concatenate([terms, terms], axis=1), read(ref, 0, 2 * CHUNK)
                )

        for chunk in range(AHEAD):
            distances(chunk)
        for chunk in range(chunks):
            if chunk + AHEAD < chunks:
                distances(chunk + AHEAD)
            if chunk >= AHEAD:
                sums(chunk - AHEAD)
            weights(chunk)
        for chunk in range(chunks - AHEAD, chunks):
            sums(chunk)
        near = near_sums[0:8, :lanes] + near_sums[8:16, :lanes] + near_sums[16:24, :lanes]
        grad = grad_sums[0:24, :lanes] + grad_sums[24:48, :lanes] + grad_sums[48:72, :lanes]

        def three(values, first):
            return [values[first + k : first + k + 1, :] for k in range(3)]

        near_vort, near_curl = three(near, 0), three(near, 3)
        grad_vort, grad_curl = three(grad, 0), three(grad, 3)
        turned = cross(where, near_vort)
        velocity = [velocity_factor * (turned[k] - near_curl[k]) for k in range(3)]
        along = vortex[0] * where[0] + vortex[1] * where[1] + vortex[2] * where[2]
        turned = cross(where, grad_vort)
        inner = [along * (turned[k] - grad_curl[k]) for k in range(3)]
        for axis in range(3):
            turned = cross(where, three(grad, 6 + 3 * axis))
            outer = three(grad, 15 + 3 * axis)
            inner = [inner[k] - vortex[axis] * (turned[k] - outer[k]) for k in range(3)]
        turned = cross(vortex, near_vort)
        stretch = [stretch_factor * (turned[k] - 5.0 * inner[k]) for k in range(3)]
        blank = jnp.zeros((2, lanes), f32)
        result = jnp.concatenate(velocity + stretch + [blank], axis=0)
        for copy in range(copies):
            store(out_ref.at[copy], result)

    if not counted:
        run(halves)
        return
    left = count_ref[0, 0] - pl.program_id(0) * halves * half
    pl.when(left > half)(functools.partial(run, halves))
    pl.when(jnp.logical_and(left > 0, left <= half))(functools.partial(run, 1))

    @pl.when(left <= 0)
    def _():
        out_ref[...] = jnp.zeros_like(out_ref)
        if moved:
            table_ref[...] = jnp.zeros_like(table_ref)


def pair_sums(table, source_sets, copies, moved=None, count=None):
    tiles, _, width = table.shape
    rows = 8
    pair = pl.BlockSpec((2, rows, width), lambda i: (i, 0, 0))
    operands, in_specs = [], []
    if count is not None:
        operands.append(count)
        in_specs.append(pl.BlockSpec(memory_space=pltpu.SMEM))
    operands.append(table)
    in_specs.append(pair)
    if moved is not None:
        operands.append(moved)
        in_specs.append(pl.BlockSpec((moved.shape[0], 2, rows, width), lambda i: (0, i, 0, 0)))
    sources = 0
    for source_set in source_sets:
        operands.extend(source_set)
        in_specs.extend([whole] * 3)
        sources += source_set[0].shape[1]
    out_shape = [jax.ShapeDtypeStruct((copies, tiles, rows, width), f32)]
    out_specs = [pl.BlockSpec((copies, 2, rows, width), lambda i: (0, i, 0, 0))]
    if moved is not None:
        out_shape.append(jax.ShapeDtypeStruct((tiles, rows, width), f32))
        out_specs.append(pair)
    pairs = sources * tiles * width
    return pl.pallas_call(
        functools.partial(pairs_kernel, len(source_sets), moved is not None, copies, count is not None),
        grid=(tiles // 2,),
        in_specs=in_specs,
        out_specs=out_specs,
        out_shape=out_shape,
        scratch_shapes=[
            pltpu.VMEM((32, 2 * width), f32),
            pltpu.VMEM((32, 2 * width), f32),
            pltpu.VMEM((80, 2 * width), f32),
        ]
        + [pltpu.VMEM((CHUNK, 2 * width), f32)] * SLOTS
        + [pltpu.VMEM((2 * CHUNK, 2 * width), bf16)] * (2 * SLOTS),
        compiler_params=pltpu.CompilerParams(vmem_limit_bytes=48 << 20),
        cost_estimate=pl.CostEstimate(
            flops=600 * pairs, bytes_accessed=300 * sources, transcendentals=pairs
        ),
    )(*operands)


def swap(values):
    return lax.all_to_all(values, "grp", split_axis=0, concat_axis=0, tiled=True)


def spread(values, groups):
    return swap(jnp.broadcast_to(values[None], (groups,) + values.shape))


def per_device(
    src_pos, src_vort, face_valid, tgt_pos, tgt_vort, mig_pos, mig_vort, mig_valid, mig_route
):
    groups = lax.axis_size("grp")
    slabs = lax.axis_size("slab")

    def components(values):
        return values.transpose(0, 2, 1, 3)[0]

    places = components(src_pos)
    vortex = components(src_vort)
    sources = places.shape[2]
    faces = face_valid.shape[3]
    own = tgt_pos.shape[3]
    slots = groups * CAP
    mine = jnp.concatenate(
        [tgt_pos[0, 0], tgt_vort[0, 0], jnp.ones((1, own), f32), jnp.zeros((1, own), f32)], axis=0
    )
    going_up, going_down = make_sends(
        places, vortex, face_valid[0, 0], components(mig_pos), components(mig_vort), mig_valid[0], mig_route[0, 0],
        2 * groups,
    )
    from_lower = lax.ppermute(going_up, "slab", [(i, (i + 1) % slabs) for i in range(slabs)])
    from_upper = lax.ppermute(going_down, "slab", [((i + 1) % slabs, i) for i in range(slabs)])
    own_set = prepare(sources, places, vortex)
    arrived = jnp.concatenate(
        [from_lower[:, faces + slots :], from_upper[:, faces : faces + slots]], axis=1
    )
    received = spread(jnp.concatenate([mine, arrived], axis=0), groups)
    face_set = prepare(2 * faces, from_lower, from_upper)
    sets = [own_set, face_set]
    (first_a,) = pair_sums(received, sets, groups)
    moved_a = swap(first_a.reshape(groups, -1, 128)).reshape(first_a.shape)
    table_b, rank, count = compact(received)
    (first_b,) = pair_sums(table_b, sets, groups, count=count)
    moved_b = swap(first_b.reshape(groups, -1, 128)).reshape(first_b.shape)
    second_a, table_a = pair_sums(received, sets, 1, moved=moved_a)
    second_b, table_b = pair_sums(table_b, sets, 1, moved=moved_b, count=count)
    rank = rank.reshape(2, groups, CAP, groups).transpose(1, 0, 3, 2).reshape(groups, 2 * slots)
    sums, table_b = expand_slots(rank, second_a[0], second_b[0], table_b)
    sums = swap(sums)
    member = lax.axis_index("grp")
    own = [lax.dynamic_index_in_dim(t, member, 0, keepdims=False) for t in (table_a, table_b)]
    total = jnp.sum(sums, axis=0)
    outs = []
    for first in (0, 3):
        moved = [
            (own[k][first : first + 3] + time_step * total[8 * k + first : 8 * k + first + 3])
            * own[k][6:7]
            for k in range(2)
        ]
        moved = jnp.concatenate([part[:, None, :] for part in moved], axis=2)
        outs.append(moved[None].transpose(0, 2, 1, 3))
    return tuple(outs)


def solution(mesh):
    return jax.shard_map(
        per_device,
        mesh=mesh,
        in_specs=(
            P("slab", "grp", None, None),
            P("slab", "grp", None, None),
            P("slab", "grp", None, None),
            P("slab", "grp", None, None),
            P("slab", "grp", None, None),
            P("slab", "grp", None, None),
            P("slab", "grp", None, None),
            P("slab", "grp", None),
            P("slab", "grp", None, None),
        ),
        out_specs=(P("slab", "grp", None, None), P("slab", "grp", None, None)),
        check_vma=False,
    )
```

```python
import functools
import math

import jax
import jax.numpy as jnp
from jax import lax
from jax.experimental import pallas as pl
from jax.experimental.pallas import tpu as pltpu
from jax.sharding import PartitionSpec as P

CAP = 8
STEPS = 2
core_square = 0.0225
time_step = 0.1
strength = 0.03 / (4.0 * math.pi)

centre = 0.5
unit_square = 1.5 * core_square
unit = math.sqrt(unit_square)
velocity_factor = -strength / unit_square
stretch_factor = -strength / (unit_square * unit)
f32 = jnp.float32
bf16 = jnp.bfloat16
whole = pl.BlockSpec(memory_space=pltpu.VMEM)


def three_pieces(values):
    high = values.astype(bf16).astype(f32)
    rest = values - high
    middle = rest.astype(bf16).astype(f32)
    low = rest - middle
    return high, middle, low


def two_pieces(values):
    high = values.astype(bf16)
    low = (values - high.astype(f32)).astype(bf16)
    return jnp.concatenate([high, low], axis=0)


def dot(left, right):
    return lax.dot_general(left, right, (((1,), (0,)), ((), ())), preferred_element_type=f32)


def cross(left, right):
    return [
        left[(k + 1) % 3] * right[(k + 2) % 3] - left[(k + 2) % 3] * right[(k + 1) % 3]
        for k in range(3)
    ]


def send_kernel(
    faces, pos_ref, vort_ref, valid_ref, mig_pos_ref, mig_vort_ref, mig_valid_ref, route_ref,
    up_ref, down_ref, record,
):
    sources = pos_ref.shape[2]
    migrants = route_ref.shape[0]
    slots = (up_ref.shape[1] - faces) // 2
    destinations = 2 * slots // CAP
    route = route_ref[...]
    matches = route == lax.broadcasted_iota(jnp.int32, (migrants, destinations), 1)
    matches = jnp.where(matches, 1.0, 0.0)
    earlier = lax.broadcasted_iota(jnp.int32, (migrants, migrants), 0) > lax.broadcasted_iota(
        jnp.int32, (migrants, migrants), 1
    )
    before = dot(jnp.where(earlier, 1.0, 0.0).astype(bf16), matches.astype(bf16))
    order = jnp.sum(before * matches, axis=1, keepdims=True).astype(jnp.int32)
    placing = (route * CAP + order) == lax.broadcasted_iota(jnp.int32, (migrants, 2 * slots), 1)
    placing = jnp.where(placing, 1.0, 0.0).astype(bf16)
    record[...] = jnp.zeros_like(record)
    for k in range(3):
        record[k : k + 1, :] = mig_pos_ref[k]
        record[3 + k : 4 + k, :] = mig_vort_ref[k]
    record[6:7, :] = mig_valid_ref[...].astype(f32)
    pieces = jnp.concatenate(three_pieces(record[...]), axis=0)
    placed = dot(jnp.concatenate([pieces, jnp.zeros((8, migrants), f32)], axis=0).astype(bf16), placing)
    placed = placed[0:8] + placed[8:16] + placed[16:24]
    first = lax.broadcasted_iota(jnp.int32, placed.shape, 0) == 0
    for ref, begin, shift, which in ((down_ref, 0, 1.0, 0), (up_ref, sources - faces, -1.0, 1)):
        piece = slice(begin, begin + faces)
        mask = valid_ref[which : which + 1, :].astype(f32)
        for k in range(3):
            place = pos_ref[k, :, piece]
            ref[k : k + 1, :faces] = place + shift if k == 0 else place
            ref[3 + k : 4 + k, :faces] = vort_ref[k, :, piece] * mask
        ref[6:8, :faces] = jnp.zeros((2, faces), f32)
        ref[:, faces:] = jnp.where(first, placed + shift, placed)


def make_sends(places, vortex, valid, mig_pos, mig_vort, mig_valid, route, destinations):
    faces = valid.shape[1]
    shape = jax.ShapeDtypeStruct((8, faces + destinations * CAP), f32)
    return pl.pallas_call(
        functools.partial(send_kernel, faces),
        in_specs=[whole] * 7,
        out_specs=[whole] * 2,
        out_shape=[shape, shape],
        scratch_shapes=[pltpu.VMEM((8, route.shape[0]), f32)],
        compiler_params=pltpu.CompilerParams(vmem_limit_bytes=62 << 20),
    )(places, vortex, valid, mig_pos, mig_vort, mig_valid, route)


def prepare_kernel(length, *refs):
    source_refs = refs[:-5]
    near_ref, grad_ref, dist_ref, rows, dist = refs[-5:]

    def columns(row):
        if source_refs[0].shape[0] == 3:
            return source_refs[row // 3][row % 3]
        return jnp.concatenate([ref[row : row + 1, : length // 2] for ref in source_refs], axis=1)

    places = [(columns(k) - centre) * (1.0 / unit) for k in range(3)]
    vortex = [columns(3 + k) for k in range(3)]
    curled = cross(places, vortex)
    for k in range(3):
        rows[k : k + 1, :] = vortex[k]
        rows[3 + k : 4 + k, :] = curled[k]
        for l in range(3):
            at = 6 + 3 * k + l
            rows[at : at + 1, :] = places[k] * vortex[l]
            rows[at + 9 : at + 10, :] = places[k] * curled[l]
    high, middle, low = three_pieces(rows[...])
    blank = jnp.zeros((8, high.shape[1]), f32)
    grad_ref[...] = jnp.concatenate([high, middle, low, blank], axis=0).astype(bf16)
    near_ref[...] = jnp.concatenate([high[0:8], middle[0:8], low[0:8], blank], axis=0).astype(bf16)
    square = places[0] * places[0] + places[1] * places[1] + places[2] * places[2]
    square_parts = three_pieces(square + core_square / unit_square)
    dist[...] = jnp.zeros_like(dist)
    for k in range(3):
        parts = three_pieces(places[k])
        for place, part in enumerate((0, 0, 1, 0, 2, 1)):
            dist[3 * place + k : 3 * place + k + 1, :] = parts[part]
        dist[18 + k : 19 + k, :] = square_parts[k]
        dist[21 + k : 22 + k, :] = jnp.ones_like(square)
    dist_ref[...] = dist[...].astype(bf16)


def prepare(length, *sources):
    return pl.pallas_call(
        functools.partial(prepare_kernel, length),
        in_specs=[whole] * len(sources),
        out_specs=[whole] * 3,
        out_shape=[
            jax.ShapeDtypeStruct((32, length), bf16),
            jax.ShapeDtypeStruct((80, length), bf16),
            jax.ShapeDtypeStruct((32, length), bf16),
        ],
        scratch_shapes=[pltpu.VMEM((24, length), f32), pltpu.VMEM((32, length), f32)],
        compiler_params=pltpu.CompilerParams(vmem_limit_bytes=48 << 20),
    )(*sources)


def compact_kernel(arrived_ref, table_ref, rank_ref, count_ref):
    groups, _, slots = arrived_ref.shape
    valid = jnp.concatenate([arrived_ref[m, 14:15, :] for m in range(groups)], axis=0)
    row = lax.broadcasted_iota(jnp.int32, (slots, slots), 0)
    column = lax.broadcasted_iota(jnp.int32, (slots, slots), 1)
    earlier = jnp.where(row < column, 1.0, 0.0).astype(bf16)
    same = jnp.where(row == column, 1.0, 0.0).astype(bf16)

    def turned(matrix, which):
        return lax.dot_general(
            matrix, which, (((0,), (1,)), ((), ())), preferred_element_type=f32
        )

    flags = valid.astype(bf16)
    within = turned(earlier, flags)
    living = turned(same, flags)
    totals = jnp.sum(living, axis=0, keepdims=True)
    ahead = [jnp.zeros((1, 1), f32)]
    for m in range(1, groups):
        ahead.append(ahead[-1] + totals[:, m - 1 : m])
    rank = jnp.where(living > 0.5, within + jnp.concatenate(ahead, axis=1), -1.0)
    rank_ref[...] = rank
    count_ref[0, 0] = jnp.sum(valid).astype(jnp.int32)
    wanted = lax.broadcasted_iota(jnp.int32, (slots, groups * slots), 1).astype(f32)
    placed = jnp.zeros((32, groups * slots), f32)
    for m in range(groups):
        pieces = three_pieces(arrived_ref[m, 8:16, :])
        pieces = jnp.concatenate(pieces + (jnp.zeros((8, slots), f32),), axis=0).astype(bf16)
        chosen = jnp.where(rank[:, m : m + 1] == wanted, 1.0, 0.0).astype(bf16)
        placed = placed + dot(pieces, chosen)
    placed = placed[0:8] + placed[8:16] + placed[16:24]
    for m in range(groups):
        table_ref[m] = placed[:, m * slots : (m + 1) * slots]


def compact(received):
    groups, _, slots = received.shape
    return pl.pallas_call(
        compact_kernel,
        in_specs=[whole],
        out_specs=[whole, whole, pl.BlockSpec(memory_space=pltpu.SMEM)],
        out_shape=[
            jax.ShapeDtypeStruct((groups, 8, slots), f32),
            jax.ShapeDtypeStruct((slots, groups), f32),
            jax.ShapeDtypeStruct((1, 1), jnp.int32),
        ],
        compiler_params=pltpu.CompilerParams(vmem_limit_bytes=48 << 20),
    )(received)


def expand_kernel(rank_ref, own_ref, moved_ref, table_ref, sums_ref, places_ref):
    groups, _, slots = moved_ref.shape
    rows = [
        jnp.concatenate([ref[m] for m in range(groups)], axis=1) for ref in (moved_ref, table_ref)
    ]
    pieces = jnp.concatenate(three_pieces(jnp.concatenate(rows, axis=0)), axis=0).astype(bf16)
    wanted = lax.broadcasted_iota(jnp.int32, (groups * slots, slots), 0).astype(f32)
    for member in range(groups):
        chosen = jnp.where(rank_ref[member : member + 1, :] == wanted, 1.0, 0.0).astype(bf16)
        found = dot(pieces, chosen)
        found = found[0:16] + found[16:32] + found[32:48]
        sums_ref[member, 0:8, :] = own_ref[member]
        sums_ref[member, 8:16, :] = found[0:8]
        places_ref[member] = found[8:16]


def expand_slots(rank, own, moved, table):
    groups, _, slots = moved.shape
    return pl.pallas_call(
        expand_kernel,
        in_specs=[whole] * 4,
        out_specs=[whole] * 2,
        out_shape=[
            jax.ShapeDtypeStruct((groups, 16, slots), f32),
            jax.ShapeDtypeStruct((groups, 8, slots), f32),
        ],
        compiler_params=pltpu.CompilerParams(vmem_limit_bytes=48 << 20),
    )(rank, own, moved, table)


CHUNK = 128
FINE = 16
SLOTS = 6
AHEAD = 3


def pairs_kernel(sets, moved, copies, counted, *refs):
    refs = list(refs)
    count_ref = refs.pop(0) if counted else None
    tgt_ref = refs.pop(0)
    moved_ref = refs.pop(0) if moved else None
    source_refs = [refs.pop(0) for _ in range(3 * sets)]
    out_ref = refs.pop(0)
    table_ref = refs.pop(0) if moved else None
    tgt, near_sums, grad_sums = refs[:3]
    held = refs[3:]
    halves, rows, half = tgt_ref.shape

    def run(parts):
        lanes = parts * half

        def joined(ref):
            return ref[0] if parts == 1 else jnp.concatenate([ref[0], ref[1]], axis=1)

        def store(ref, values):
            for part in range(halves):
                at = slice(part * half, part * half + half)
                ref[part] = values[:, at] if part < parts else jnp.zeros((rows, half), f32)

        table = joined(tgt_ref)
        if moved:
            step = joined(moved_ref.at[0])
            for sender in range(1, moved_ref.shape[0]):
                step = step + joined(moved_ref.at[sender])
            table = table + time_step * step
            store(table_ref, table)
        where = [(table[k : k + 1, :] - centre) * (1.0 / unit) for k in range(3)]
        vortex = [table[3 + k : 4 + k, :] for k in range(3)]
        square = where[0] * where[0] + where[1] * where[1] + where[2] * where[2]
        square_parts = three_pieces(square)
        tgt[...] = jnp.zeros_like(tgt)
        for k in range(3):
            pieces = three_pieces(-2.0 * where[k])
            for place, piece in enumerate((0, 1, 0, 2, 0, 1)):
                tgt[3 * place + k : 3 * place + k + 1, :lanes] = pieces[piece]
            tgt[18 + k : 19 + k, :lanes] = jnp.ones_like(square)
            tgt[21 + k : 22 + k, :lanes] = square_parts[k]
        targets = tgt[:, :lanes].astype(bf16)
        near_sums[...] = jnp.zeros_like(near_sums)
        grad_sums[...] = jnp.zeros_like(grad_sums)
        start = jnp.minimum(pl.program_id(0), 0)
        per_set = source_refs[0].shape[1] // CHUNK
        chunks = sets * per_set

        def source(which, chunk):
            number, place = divmod(chunk, per_set)
            return source_refs[3 * number + which][:, place * CHUNK : (place + 1) * CHUNK]

        def read(ref, at, count):
            return ref[pl.ds(pl.multiple_of(start * CHUNK + at, count), count), :lanes]

        def distances(chunk):
            held[chunk % SLOTS][:, :lanes] = lax.dot_general(
                source(2, chunk), targets, (((0,), (0,)), ((), ())), preferred_element_type=f32
            )

        def weights(chunk):
            distance_ref = held[chunk % SLOTS]
            near_ref = held[SLOTS + chunk % SLOTS]
            grad_ref = held[2 * SLOTS + chunk % SLOTS]
            for at in range(0, CHUNK, FINE):
                root = lax.rsqrt(read(distance_ref, at, FINE))
                square_inv = root * root
                third = square_inv * root
                fifth = third * square_inv
                for ref, weight in (
                    (near_ref, third + fifth),
                    (grad_ref, fifth * (square_inv + 0.6)),
                ):
                    high = weight.astype(bf16)
                    ref[at : at + FINE, :lanes] = high
                    low = (weight - high.astype(f32)).astype(bf16)
                    ref[CHUNK + at : CHUNK + at + FINE, :lanes] = low

        def sums(chunk):
            for which, total in ((0, near_sums), (1, grad_sums)):
                ref = held[(1 + which) * SLOTS + chunk % SLOTS]
                terms = source(which, chunk)
                total[:, :lanes] += dot(
                    jnp.concatenate([terms, terms], axis=1), read(ref, 0, 2 * CHUNK)
                )

        for chunk in range(AHEAD):
            distances(chunk)
        for chunk in range(chunks):
            if chunk + AHEAD < chunks:
                distances(chunk + AHEAD)
            if chunk >= AHEAD:
                sums(chunk - AHEAD)
            weights(chunk)
        for chunk in range(chunks - AHEAD, chunks):
            sums(chunk)
        near = near_sums[0:8, :lanes] + near_sums[8:16, :lanes] + near_sums[16:24, :lanes]
        grad = grad_sums[0:24, :lanes] + grad_sums[24:48, :lanes] + grad_sums[48:72, :lanes]

        def three(values, first):
            return [values[first + k : first + k + 1, :] for k in range(3)]

        near_vort, near_curl = three(near, 0), three(near, 3)
        grad_vort, grad_curl = three(grad, 0), three(grad, 3)
        turned = cross(where, near_vort)
        velocity = [velocity_factor * (turned[k] - near_curl[k]) for k in range(3)]
        along = vortex[0] * where[0] + vortex[1] * where[1] + vortex[2] * where[2]
        turned = cross(where, grad_vort)
        inner = [along * (turned[k] - grad_curl[k]) for k in range(3)]
        for axis in range(3):
            turned = cross(where, three(grad, 6 + 3 * axis))
            outer = three(grad, 15 + 3 * axis)
            inner = [inner[k] - vortex[axis] * (turned[k] - outer[k]) for k in range(3)]
        turned = cross(vortex, near_vort)
        stretch = [stretch_factor * (turned[k] - 5.0 * inner[k]) for k in range(3)]
        blank = jnp.zeros((2, lanes), f32)
        result = jnp.concatenate(velocity + stretch + [blank], axis=0)
        for copy in range(copies):
            store(out_ref.at[copy], result)

    if not counted:
        run(halves)
        return
    left = count_ref[0, 0] - pl.program_id(0) * halves * half
    pl.when(left > half)(functools.partial(run, halves))
    pl.when(jnp.logical_and(left > 0, left <= half))(functools.partial(run, 1))

    @pl.when(left <= 0)
    def _():
        out_ref[...] = jnp.zeros_like(out_ref)
        if moved:
            table_ref[...] = jnp.zeros_like(table_ref)


def pair_sums(table, source_sets, copies, moved=None, count=None):
    tiles, _, width = table.shape
    rows = 8
    pair = pl.BlockSpec((2, rows, width), lambda i: (i, 0, 0))
    operands, in_specs = [], []
    if count is not None:
        operands.append(count)
        in_specs.append(pl.BlockSpec(memory_space=pltpu.SMEM))
    operands.append(table)
    in_specs.append(pair)
    if moved is not None:
        operands.append(moved)
        in_specs.append(pl.BlockSpec((moved.shape[0], 2, rows, width), lambda i: (0, i, 0, 0)))
    sources = 0
    for source_set in source_sets:
        operands.extend(source_set)
        in_specs.extend([whole] * 3)
        sources += source_set[0].shape[1]
    out_shape = [jax.ShapeDtypeStruct((copies, tiles, rows, width), f32)]
    out_specs = [pl.BlockSpec((copies, 2, rows, width), lambda i: (0, i, 0, 0))]
    if moved is not None:
        out_shape.append(jax.ShapeDtypeStruct((tiles, rows, width), f32))
        out_specs.append(pair)
    pairs = sources * tiles * width
    return pl.pallas_call(
        functools.partial(pairs_kernel, len(source_sets), moved is not None, copies, count is not None),
        grid=(tiles // 2,),
        in_specs=in_specs,
        out_specs=out_specs,
        out_shape=out_shape,
        scratch_shapes=[
            pltpu.VMEM((32, 2 * width), f32),
            pltpu.VMEM((32, 2 * width), f32),
            pltpu.VMEM((80, 2 * width), f32),
        ]
        + [pltpu.VMEM((CHUNK, 2 * width), f32)] * SLOTS
        + [pltpu.VMEM((2 * CHUNK, 2 * width), bf16)] * (2 * SLOTS),
        compiler_params=pltpu.CompilerParams(vmem_limit_bytes=48 << 20),
        cost_estimate=pl.CostEstimate(
            flops=600 * pairs, bytes_accessed=300 * sources, transcendentals=pairs
        ),
    )(*operands)


def swap(values):
    return lax.all_to_all(values, "grp", split_axis=0, concat_axis=0, tiled=True)


def spread(values, groups):
    return swap(jnp.broadcast_to(values[None], (groups,) + values.shape))


def per_device(
    src_pos, src_vort, face_valid, tgt_pos, tgt_vort, mig_pos, mig_vort, mig_valid, mig_route
):
    groups = lax.axis_size("grp")
    slabs = lax.axis_size("slab")

    def components(values):
        return values.transpose(0, 2, 1, 3)[0]

    places = components(src_pos)
    vortex = components(src_vort)
    sources = places.shape[2]
    faces = face_valid.shape[3]
    own = tgt_pos.shape[3]
    slots = groups * CAP
    mine = jnp.concatenate(
        [tgt_pos[0, 0], tgt_vort[0, 0], jnp.ones((1, own), f32), jnp.zeros((1, own), f32)], axis=0
    )
    going_up, going_down = make_sends(
        places, vortex, face_valid[0, 0], components(mig_pos), components(mig_vort), mig_valid[0], mig_route[0, 0],
        2 * groups,
    )
    from_lower = lax.ppermute(going_up, "slab", [(i, (i + 1) % slabs) for i in range(slabs)])
    from_upper = lax.ppermute(going_down, "slab", [((i + 1) % slabs, i) for i in range(slabs)])
    own_set = prepare(sources, places, vortex)
    arrived = jnp.concatenate(
        [from_lower[:, faces + slots :], from_upper[:, faces : faces + slots]], axis=1
    )
    received = spread(jnp.concatenate([mine, arrived], axis=0), groups)
    face_set = prepare(2 * faces, from_lower, from_upper)
    sets = [own_set, face_set]
    (first_a,) = pair_sums(received, sets, groups)
    moved_a = swap(first_a.reshape(groups, -1, 128)).reshape(first_a.shape)
    table_b, rank, count = compact(received)
    (first_b,) = pair_sums(table_b, sets, groups, count=count)
    moved_b = swap(first_b.reshape(groups, -1, 128)).reshape(first_b.shape)
    second_a, table_a = pair_sums(received, sets, 1, moved=moved_a)
    second_b, table_b = pair_sums(table_b, sets, 1, moved=moved_b, count=count)
    rank = rank.reshape(2, groups, CAP, groups).transpose(1, 0, 3, 2).reshape(groups, 2 * slots)
    sums, table_b = expand_slots(rank, second_a[0], second_b[0], table_b)
    sums = swap(sums)
    member = lax.axis_index("grp")
    own = [lax.dynamic_index_in_dim(t, member, 0, keepdims=False) for t in (table_a, table_b)]
    total = jnp.sum(sums, axis=0)
    outs = []
    for first in (0, 3):
        moved = [
            (own[k][first : first + 3] + time_step * total[8 * k + first : 8 * k + first + 3])
            * own[k][6:7]
            for k in range(2)
        ]
        moved = jnp.concatenate([part[:, None, :] for part in moved], axis=2)
        outs.append(moved[None].transpose(0, 2, 1, 3))
    return tuple(outs)


def solution(mesh):
    return jax.shard_map(
        per_device,
        mesh=mesh,
        in_specs=(
            P("slab", "grp", None, None),
            P("slab", "grp", None, None),
            P("slab", "grp", None, None),
            P("slab", "grp", None, None),
            P("slab", "grp", None, None),
            P("slab", "grp", None, None),
            P("slab", "grp", None, None),
            P("slab", "grp", None),
            P("slab", "grp", None, None),
        ),
        out_specs=(P("slab", "grp", None, None), P("slab", "grp", None, None)),
        check_vma=False,
    )
```

```python
import functools
import math

import jax
import jax.numpy as jnp
from jax import lax
from jax.experimental import pallas as pl
from jax.experimental.pallas import tpu as pltpu
from jax.sharding import PartitionSpec as P

CAP = 8
STEPS = 2
core_square = 0.0225
time_step = 0.1
strength = 0.03 / (4.0 * math.pi)

centre = 0.5
unit_square = 1.5 * core_square
unit = math.sqrt(unit_square)
velocity_factor = -strength / unit_square
stretch_factor = -strength / (unit_square * unit)
f32 = jnp.float32
bf16 = jnp.bfloat16
whole = pl.BlockSpec(memory_space=pltpu.VMEM)


def three_pieces(values):
    high = values.astype(bf16).astype(f32)
    rest = values - high
    middle = rest.astype(bf16).astype(f32)
    low = rest - middle
    return high, middle, low


def two_pieces(values):
    high = values.astype(bf16)
    low = (values - high.astype(f32)).astype(bf16)
    return jnp.concatenate([high, low], axis=0)


def dot(left, right):
    return lax.dot_general(left, right, (((1,), (0,)), ((), ())), preferred_element_type=f32)


def cross(left, right):
    return [
        left[(k + 1) % 3] * right[(k + 2) % 3] - left[(k + 2) % 3] * right[(k + 1) % 3]
        for k in range(3)
    ]


def send_kernel(
    faces, pos_ref, vort_ref, valid_ref, mig_pos_ref, mig_vort_ref, mig_valid_ref, route_ref,
    up_ref, down_ref, record,
):
    sources = pos_ref.shape[1]
    migrants = route_ref.shape[0]
    slots = (up_ref.shape[1] - faces) // 2
    destinations = 2 * slots // CAP
    route = route_ref[...]
    matches = route == lax.broadcasted_iota(jnp.int32, (migrants, destinations), 1)
    matches = jnp.where(matches, 1.0, 0.0)
    earlier = lax.broadcasted_iota(jnp.int32, (migrants, migrants), 0) > lax.broadcasted_iota(
        jnp.int32, (migrants, migrants), 1
    )
    before = dot(jnp.where(earlier, 1.0, 0.0).astype(bf16), matches.astype(bf16))
    order = jnp.sum(before * matches, axis=1, keepdims=True).astype(jnp.int32)
    placing = (route * CAP + order) == lax.broadcasted_iota(jnp.int32, (migrants, 2 * slots), 1)
    placing = jnp.where(placing, 1.0, 0.0).astype(bf16)
    record[...] = jnp.zeros_like(record)
    record[0:3, :] = mig_pos_ref[...]
    record[3:6, :] = mig_vort_ref[...]
    record[6:7, :] = mig_valid_ref[...].astype(f32)
    pieces = jnp.concatenate(three_pieces(record[...]), axis=0)
    placed = dot(jnp.concatenate([pieces, jnp.zeros((8, migrants), f32)], axis=0).astype(bf16), placing)
    placed = placed[0:8] + placed[8:16] + placed[16:24]
    first = lax.broadcasted_iota(jnp.int32, placed.shape, 0) == 0
    for ref, begin, shift, which in ((down_ref, 0, 1.0, 0), (up_ref, sources - faces, -1.0, 1)):
        piece = slice(begin, begin + faces)
        mask = valid_ref[which : which + 1, :].astype(f32)
        ref[0:1, :faces] = pos_ref[0:1, piece] + shift
        ref[1:3, :faces] = pos_ref[1:3, piece]
        ref[3:6, :faces] = vort_ref[:, piece] * mask
        ref[6:8, :faces] = jnp.zeros((2, faces), f32)
        ref[:, faces:] = jnp.where(first, placed + shift, placed)


def make_sends(places, vortex, valid, mig_pos, mig_vort, mig_valid, route, destinations):
    faces = valid.shape[1]
    shape = jax.ShapeDtypeStruct((8, faces + destinations * CAP), f32)
    return pl.pallas_call(
        functools.partial(send_kernel, faces),
        in_specs=[whole] * 7,
        out_specs=[whole] * 2,
        out_shape=[shape, shape],
        scratch_shapes=[pltpu.VMEM((8, route.shape[0]), f32)],
        compiler_params=pltpu.CompilerParams(vmem_limit_bytes=48 << 20),
    )(places, vortex, valid, mig_pos, mig_vort, mig_valid, route)


def prepare_kernel(length, *refs):
    source_refs = refs[:-5]
    near_ref, grad_ref, dist_ref, rows, dist = refs[-5:]

    def columns(row):
        if source_refs[0].shape[0] == 3:
            return source_refs[row // 3][row % 3 : row % 3 + 1, :]
        return jnp.concatenate([ref[row : row + 1, : length // 2] for ref in source_refs], axis=1)

    places = [(columns(k) - centre) * (1.0 / unit) for k in range(3)]
    vortex = [columns(3 + k) for k in range(3)]
    curled = cross(places, vortex)
    for k in range(3):
        rows[k : k + 1, :] = vortex[k]
        rows[3 + k : 4 + k, :] = curled[k]
        for l in range(3):
            at = 6 + 3 * k + l
            rows[at : at + 1, :] = places[k] * vortex[l]
            rows[at + 9 : at + 10, :] = places[k] * curled[l]
    high, middle, low = three_pieces(rows[...])
    blank = jnp.zeros((8, high.shape[1]), f32)
    grad_ref[...] = jnp.concatenate([high, middle, low, blank], axis=0).astype(bf16)
    near_ref[...] = jnp.concatenate([high[0:8], middle[0:8], low[0:8], blank], axis=0).astype(bf16)
    square = places[0] * places[0] + places[1] * places[1] + places[2] * places[2]
    square_parts = three_pieces(square + core_square / unit_square)
    dist[...] = jnp.zeros_like(dist)
    for k in range(3):
        parts = three_pieces(places[k])
        for place, part in enumerate((0, 0, 1, 0, 2, 1)):
            dist[3 * place + k : 3 * place + k + 1, :] = parts[part]
        dist[18 + k : 19 + k, :] = square_parts[k]
        dist[21 + k : 22 + k, :] = jnp.ones_like(square)
    dist_ref[...] = dist[...].astype(bf16)


def prepare(length, *sources):
    return pl.pallas_call(
        functools.partial(prepare_kernel, length),
        in_specs=[whole] * len(sources),
        out_specs=[whole] * 3,
        out_shape=[
            jax.ShapeDtypeStruct((32, length), bf16),
            jax.ShapeDtypeStruct((80, length), bf16),
            jax.ShapeDtypeStruct((32, length), bf16),
        ],
        scratch_shapes=[pltpu.VMEM((24, length), f32), pltpu.VMEM((32, length), f32)],
        compiler_params=pltpu.CompilerParams(vmem_limit_bytes=48 << 20),
    )(*sources)


def compact_kernel(arrived_ref, table_ref, rank_ref, count_ref):
    groups, _, slots = arrived_ref.shape
    valid = jnp.concatenate([arrived_ref[m, 14:15, :] for m in range(groups)], axis=0)
    row = lax.broadcasted_iota(jnp.int32, (slots, slots), 0)
    column = lax.broadcasted_iota(jnp.int32, (slots, slots), 1)
    earlier = jnp.where(row < column, 1.0, 0.0).astype(bf16)
    same = jnp.where(row == column, 1.0, 0.0).astype(bf16)

    def turned(matrix, which):
        return lax.dot_general(
            matrix, which, (((0,), (1,)), ((), ())), preferred_element_type=f32
        )

    flags = valid.astype(bf16)
    within = turned(earlier, flags)
    living = turned(same, flags)
    totals = jnp.sum(living, axis=0, keepdims=True)
    ahead = [jnp.zeros((1, 1), f32)]
    for m in range(1, groups):
        ahead.append(ahead[-1] + totals[:, m - 1 : m])
    rank = jnp.where(living > 0.5, within + jnp.concatenate(ahead, axis=1), -1.0)
    rank_ref[...] = rank
    count_ref[0, 0] = jnp.sum(valid).astype(jnp.int32)
    wanted = lax.broadcasted_iota(jnp.int32, (slots, groups * slots), 1).astype(f32)
    placed = jnp.zeros((32, groups * slots), f32)
    for m in range(groups):
        pieces = three_pieces(arrived_ref[m, 8:16, :])
        pieces = jnp.concatenate(pieces + (jnp.zeros((8, slots), f32),), axis=0).astype(bf16)
        chosen = jnp.where(rank[:, m : m + 1] == wanted, 1.0, 0.0).astype(bf16)
        placed = placed + dot(pieces, chosen)
    placed = placed[0:8] + placed[8:16] + placed[16:24]
    for m in range(groups):
        table_ref[m] = placed[:, m * slots : (m + 1) * slots]


def compact(received):
    groups, _, slots = received.shape
    return pl.pallas_call(
        compact_kernel,
        in_specs=[whole],
        out_specs=[whole, whole, pl.BlockSpec(memory_space=pltpu.SMEM)],
        out_shape=[
            jax.ShapeDtypeStruct((groups, 8, slots), f32),
            jax.ShapeDtypeStruct((slots, groups), f32),
            jax.ShapeDtypeStruct((1, 1), jnp.int32),
        ],
        compiler_params=pltpu.CompilerParams(vmem_limit_bytes=48 << 20),
    )(received)


def expand_kernel(rank_ref, own_ref, moved_ref, table_ref, sums_ref, places_ref):
    groups, _, slots = moved_ref.shape
    rows = [
        jnp.concatenate([ref[m] for m in range(groups)], axis=1) for ref in (moved_ref, table_ref)
    ]
    pieces = jnp.concatenate(three_pieces(jnp.concatenate(rows, axis=0)), axis=0).astype(bf16)
    wanted = lax.broadcasted_iota(jnp.int32, (groups * slots, slots), 0).astype(f32)
    for member in range(groups):
        chosen = jnp.where(rank_ref[member : member + 1, :] == wanted, 1.0, 0.0).astype(bf16)
        found = dot(pieces, chosen)
        found = found[0:16] + found[16:32] + found[32:48]
        sums_ref[member, 0:8, :] = own_ref[member]
        sums_ref[member, 8:16, :] = found[0:8]
        places_ref[member] = found[8:16]


def expand_slots(rank, own, moved, table):
    groups, _, slots = moved.shape
    return pl.pallas_call(
        expand_kernel,
        in_specs=[whole] * 4,
        out_specs=[whole] * 2,
        out_shape=[
            jax.ShapeDtypeStruct((groups, 16, slots), f32),
            jax.ShapeDtypeStruct((groups, 8, slots), f32),
        ],
        compiler_params=pltpu.CompilerParams(vmem_limit_bytes=48 << 20),
    )(rank, own, moved, table)


CHUNK = 128
FINE = 16
SLOTS = 6
AHEAD = 3


def pairs_kernel(sets, moved, copies, counted, *refs):
    refs = list(refs)
    count_ref = refs.pop(0) if counted else None
    tgt_ref = refs.pop(0)
    moved_ref = refs.pop(0) if moved else None
    source_refs = [refs.pop(0) for _ in range(3 * sets)]
    out_ref = refs.pop(0)
    table_ref = refs.pop(0) if moved else None
    tgt, near_sums, grad_sums = refs[:3]
    held = refs[3:]
    halves, rows, half = tgt_ref.shape

    def run(parts):
        lanes = parts * half

        def joined(ref):
            return ref[0] if parts == 1 else jnp.concatenate([ref[0], ref[1]], axis=1)

        def store(ref, values):
            for part in range(halves):
                at = slice(part * half, part * half + half)
                ref[part] = values[:, at] if part < parts else jnp.zeros((rows, half), f32)

        table = joined(tgt_ref)
        if moved:
            step = joined(moved_ref.at[0])
            for sender in range(1, moved_ref.shape[0]):
                step = step + joined(moved_ref.at[sender])
            table = table + time_step * step
            store(table_ref, table)
        where = [(table[k : k + 1, :] - centre) * (1.0 / unit) for k in range(3)]
        vortex = [table[3 + k : 4 + k, :] for k in range(3)]
        square = where[0] * where[0] + where[1] * where[1] + where[2] * where[2]
        square_parts = three_pieces(square)
        tgt[...] = jnp.zeros_like(tgt)
        for k in range(3):
            pieces = three_pieces(-2.0 * where[k])
            for place, piece in enumerate((0, 1, 0, 2, 0, 1)):
                tgt[3 * place + k : 3 * place + k + 1, :lanes] = pieces[piece]
            tgt[18 + k : 19 + k, :lanes] = jnp.ones_like(square)
            tgt[21 + k : 22 + k, :lanes] = square_parts[k]
        targets = tgt[:, :lanes].astype(bf16)
        near_sums[...] = jnp.zeros_like(near_sums)
        grad_sums[...] = jnp.zeros_like(grad_sums)
        start = jnp.minimum(pl.program_id(0), 0)
        per_set = source_refs[0].shape[1] // CHUNK
        chunks = sets * per_set

        def source(which, chunk):
            number, place = divmod(chunk, per_set)
            return source_refs[3 * number + which][:, place * CHUNK : (place + 1) * CHUNK]

        def read(ref, at, count):
            return ref[pl.ds(pl.multiple_of(start * CHUNK + at, count), count), :lanes]

        def distances(chunk):
            held[chunk % SLOTS][:, :lanes] = lax.dot_general(
                source(2, chunk), targets, (((0,), (0,)), ((), ())), preferred_element_type=f32
            )

        def weights(chunk):
            distance_ref = held[chunk % SLOTS]
            near_ref = held[SLOTS + chunk % SLOTS]
            grad_ref = held[2 * SLOTS + chunk % SLOTS]
            for at in range(0, CHUNK, FINE):
                root = lax.rsqrt(read(distance_ref, at, FINE))
                square_inv = root * root
                third = square_inv * root
                fifth = third * square_inv
                for ref, weight in (
                    (near_ref, third + fifth),
                    (grad_ref, fifth * (square_inv + 0.6)),
                ):
                    high = weight.astype(bf16)
                    ref[at : at + FINE, :lanes] = high
                    low = (weight - high.astype(f32)).astype(bf16)
                    ref[CHUNK + at : CHUNK + at + FINE, :lanes] = low

        def sums(chunk):
            for which, total in ((0, near_sums), (1, grad_sums)):
                ref = held[(1 + which) * SLOTS + chunk % SLOTS]
                terms = source(which, chunk)
                total[:, :lanes] += dot(
                    jnp.concatenate([terms, terms], axis=1), read(ref, 0, 2 * CHUNK)
                )

        for chunk in range(AHEAD):
            distances(chunk)
        for chunk in range(chunks):
            if chunk + AHEAD < chunks:
                distances(chunk + AHEAD)
            if chunk >= AHEAD:
                sums(chunk - AHEAD)
            weights(chunk)
        for chunk in range(chunks - AHEAD, chunks):
            sums(chunk)
        near = near_sums[0:8, :lanes] + near_sums[8:16, :lanes] + near_sums[16:24, :lanes]
        grad = grad_sums[0:24, :lanes] + grad_sums[24:48, :lanes] + grad_sums[48:72, :lanes]

        def three(values, first):
            return [values[first + k : first + k + 1, :] for k in range(3)]

        near_vort, near_curl = three(near, 0), three(near, 3)
        grad_vort, grad_curl = three(grad, 0), three(grad, 3)
        turned = cross(where, near_vort)
        velocity = [velocity_factor * (turned[k] - near_curl[k]) for k in range(3)]
        along = vortex[0] * where[0] + vortex[1] * where[1] + vortex[2] * where[2]
        turned = cross(where, grad_vort)
        inner = [along * (turned[k] - grad_curl[k]) for k in range(3)]
        for axis in range(3):
            turned = cross(where, three(grad, 6 + 3 * axis))
            outer = three(grad, 15 + 3 * axis)
            inner = [inner[k] - vortex[axis] * (turned[k] - outer[k]) for k in range(3)]
        turned = cross(vortex, near_vort)
        stretch = [stretch_factor * (turned[k] - 5.0 * inner[k]) for k in range(3)]
        blank = jnp.zeros((2, lanes), f32)
        result = jnp.concatenate(velocity + stretch + [blank], axis=0)
        for copy in range(copies):
            store(out_ref.at[copy], result)

    if not counted:
        run(halves)
        return
    left = count_ref[0, 0] - pl.program_id(0) * halves * half
    pl.when(left > half)(functools.partial(run, halves))
    pl.when(jnp.logical_and(left > 0, left <= half))(functools.partial(run, 1))

    @pl.when(left <= 0)
    def _():
        out_ref[...] = jnp.zeros_like(out_ref)
        if moved:
            table_ref[...] = jnp.zeros_like(table_ref)


def pair_sums(table, source_sets, copies, moved=None, count=None):
    tiles, _, width = table.shape
    rows = 8
    pair = pl.BlockSpec((2, rows, width), lambda i: (i, 0, 0))
    operands, in_specs = [], []
    if count is not None:
        operands.append(count)
        in_specs.append(pl.BlockSpec(memory_space=pltpu.SMEM))
    operands.append(table)
    in_specs.append(pair)
    if moved is not None:
        operands.append(moved)
        in_specs.append(pl.BlockSpec((moved.shape[0], 2, rows, width), lambda i: (0, i, 0, 0)))
    sources = 0
    for source_set in source_sets:
        operands.extend(source_set)
        in_specs.extend([whole] * 3)
        sources += source_set[0].shape[1]
    out_shape = [jax.ShapeDtypeStruct((copies, tiles, rows, width), f32)]
    out_specs = [pl.BlockSpec((copies, 2, rows, width), lambda i: (0, i, 0, 0))]
    if moved is not None:
        out_shape.append(jax.ShapeDtypeStruct((tiles, rows, width), f32))
        out_specs.append(pair)
    pairs = sources * tiles * width
    return pl.pallas_call(
        functools.partial(pairs_kernel, len(source_sets), moved is not None, copies, count is not None),
        grid=(tiles // 2,),
        in_specs=in_specs,
        out_specs=out_specs,
        out_shape=out_shape,
        scratch_shapes=[
            pltpu.VMEM((32, 2 * width), f32),
            pltpu.VMEM((32, 2 * width), f32),
            pltpu.VMEM((80, 2 * width), f32),
        ]
        + [pltpu.VMEM((CHUNK, 2 * width), f32)] * SLOTS
        + [pltpu.VMEM((2 * CHUNK, 2 * width), bf16)] * (2 * SLOTS),
        compiler_params=pltpu.CompilerParams(vmem_limit_bytes=48 << 20),
        cost_estimate=pl.CostEstimate(
            flops=600 * pairs, bytes_accessed=300 * sources, transcendentals=pairs
        ),
    )(*operands)


def swap(values):
    return lax.all_to_all(values, "grp", split_axis=0, concat_axis=0, tiled=True)


def spread(values, groups):
    return swap(jnp.broadcast_to(values[None], (groups,) + values.shape))


def per_device(
    src_pos, src_vort, face_valid, tgt_pos, tgt_vort, mig_pos, mig_vort, mig_valid, mig_route
):
    groups = lax.axis_size("grp")
    slabs = lax.axis_size("slab")
    places = src_pos[0, 0]
    vortex = src_vort[0, 0]
    sources = places.shape[1]
    faces = face_valid.shape[3]
    own = tgt_pos.shape[3]
    slots = groups * CAP
    mine = jnp.concatenate(
        [tgt_pos[0, 0], tgt_vort[0, 0], jnp.ones((1, own), f32), jnp.zeros((1, own), f32)], axis=0
    )
    going_up, going_down = make_sends(
        places, vortex, face_valid[0, 0], mig_pos[0, 0], mig_vort[0, 0], mig_valid[0], mig_route[0, 0],
        2 * groups,
    )
    from_lower = lax.ppermute(going_up, "slab", [(i, (i + 1) % slabs) for i in range(slabs)])
    from_upper = lax.ppermute(going_down, "slab", [((i + 1) % slabs, i) for i in range(slabs)])
    own_set = prepare(sources, places, vortex)
    arrived = jnp.concatenate(
        [from_lower[:, faces + slots :], from_upper[:, faces : faces + slots]], axis=1
    )
    received = spread(jnp.concatenate([mine, arrived], axis=0), groups)
    face_set = prepare(2 * faces, from_lower, from_upper)
    sets = [own_set, face_set]
    (first_a,) = pair_sums(received, sets, groups)
    moved_a = swap(first_a.reshape(groups, -1, 128)).reshape(first_a.shape)
    table_b, rank, count = compact(received)
    (first_b,) = pair_sums(table_b, sets, groups, count=count)
    moved_b = swap(first_b.reshape(groups, -1, 128)).reshape(first_b.shape)
    second_a, table_a = pair_sums(received, sets, 1, moved=moved_a)
    second_b, table_b = pair_sums(table_b, sets, 1, moved=moved_b, count=count)
    rank = rank.reshape(2, groups, CAP, groups).transpose(1, 0, 3, 2).reshape(groups, 2 * slots)
    sums, table_b = expand_slots(rank, second_a[0], second_b[0], table_b)
    sums = swap(sums)
    member = lax.axis_index("grp")
    own = [lax.dynamic_index_in_dim(t, member, 0, keepdims=False) for t in (table_a, table_b)]
    total = jnp.sum(sums, axis=0)
    outs = []
    for first in (0, 3):
        moved = [
            (own[k][first : first + 3] + time_step * total[8 * k + first : 8 * k + first + 3])
            * own[k][6:7]
            for k in range(2)
        ]
        outs.append(jnp.concatenate(moved, axis=1)[None, None])
    return tuple(outs)


def solution(mesh):
    return jax.shard_map(
        per_device,
        mesh=mesh,
        in_specs=(
            P("slab", "grp", None, None),
            P("slab", "grp", None, None),
            P("slab", "grp", None, None),
            P("slab", "grp", None, None),
            P("slab", "grp", None, None),
            P("slab", "grp", None, None),
            P("slab", "grp", None, None),
            P("slab", "grp", None),
            P("slab", "grp", None, None),
        ),
        out_specs=(P("slab", "grp", None, None), P("slab", "grp", None, None)),
        check_vma=False,
    )
```
